128 devices in a mesh: pair: 16 (over z, x), slab: 8 (over y, core).
Axes of the slice: x: 4, y: 4, z: 4, core: 2. Of those that a mesh axis runs over, the one named last changes fastest.
Arguments:
- amplitudes: bfloat16 [16, 8, 512, 512], P('pair', 'slab'), may hold values from -6 to 6
- integrals: bfloat16 [8, 16, 512, 512], P(None, 'pair', 'slab'), may hold values from -0.25 to 0.25
- occ_irrep: int32 [16, 1], replicated, may hold values from 0 to 7
- slab_irrep: int32 [8], replicated, may hold values from 0 to 7, each once
- virt_irrep: int32 [512, 1], replicated, may hold values from 0 to 7
Outputs:
- residual: float32 [16, 16, 512, 512], P('pair', None, 'slab')
The draws below stay inside these ranges and needn't reach their ends.
Inputs may be any that keep to these rules, and one draw needn't show every extreme that they name: `occ_irrep`: D2h irrep labels; the product of two irreps is the bitwise exclusive or of their labels; every label appears among the 16 window orbitals, among the 512 virtuals, and exactly once among the 8 slab orbitals.
All inputs are finite; a program needn't handle non-finite values.
Results may differ from the reference program's by a relative error of at most 0.0003.
Values may be sent and summed in bfloat16 or wider, within the bound.
A program may use at most 64 MiB of HBM per device.

```python
import jax
import jax.numpy as jnp
from jax import lax

V = 512
K = 8
NO = 16


def block_levels(stream_key, dims, pieces, least, largest):
    gain = 1.0
    for axis_at, shards_of in pieces:
        steps = jax.random.uniform(jax.random.fold_in(jax.random.fold_in(stream_key, 6), axis_at), (shards_of,), jnp.float32, least / len(pieces), largest / len(pieces))
        gain = gain * jnp.repeat(jnp.exp(steps), dims[axis_at] // shards_of).reshape((-1,) + (1,) * (len(dims) - 1 - axis_at))
    return gain


def different_ones(stream_key, rows, amount, top, lift):
    order = jax.random.permutation(jax.random.fold_in(stream_key, 1), amount)
    boost = order
    for power in range(3):
        boost = boost * boost // amount
    boost = boost * lift // amount
    chance = jax.random.randint(jax.random.fold_in(stream_key, 2), (rows, amount), 0, 4096) + boost
    fixed_rows = jax.random.permutation(jax.random.fold_in(stream_key, 3), rows)[jnp.arange(amount) % rows]
    chance = jnp.where(jnp.arange(rows)[:, None] == fixed_rows[None, :], 1 << 14, chance)
    score = chance * amount + jnp.arange(amount)
    return lax.top_k(score.astype(jnp.int32), top)[1].astype(jnp.int32)


def gaussian(own_key, dims, spread, limit, shards=(), kind=jnp.bfloat16):
    result = jax.random.normal(own_key, dims, jnp.float32) * spread
    if len(shards) > 0:
        result = block_levels(own_key, dims, shards, -0.22, 0.18) * result
    return jnp.clip(result, min=-limit, max=limit).astype(kind)


def setup_inputs(seed: int = 0) -> dict:
    key_list = jax.random.split(jax.random.key(seed), 6)
    return {
        "amplitudes": gaussian(key_list[0], (NO, K, V, V), 1.0, 6.0, ((0, 16), (1, 8))),
        "integrals": gaussian(key_list[1], (K, NO, V, V), (K * V // 8) ** -0.5, 0.25, ((1, 16), (2, 8))),
        "occ_irrep": different_ones(key_list[2], NO, 8, 1, 1024),
        "slab_irrep": jax.random.permutation(key_list[3], 8).astype(jnp.int32),
        "virt_irrep": different_ones(key_list[4], V, 8, 1, 2048),
    }


def reference(amplitudes, integrals, occ_irrep, slab_irrep, virt_irrep):
    occ_labels = occ_irrep[:, 0]
    virt_labels = virt_irrep[:, 0]
    occ_slab = jnp.bitwise_xor(occ_labels[:, None], slab_irrep[None, :])
    virt_pairs = jnp.bitwise_xor(virt_labels[:, None], virt_labels[None, :])
    allowed = occ_slab[:, :, None, None] == virt_pairs[None, None, :, :]
    sym_amps = amplitudes * allowed.astype(amplitudes.dtype)
    slab_occ = jnp.bitwise_xor(slab_irrep[:, None], occ_labels[None, :])
    int_allowed = slab_occ[:, :, None, None] == virt_pairs[None, None, :, :]
    sym_ints = integrals * int_allowed.astype(integrals.dtype)
    left_side = jnp.transpose(sym_amps, (0, 2, 1, 3)).reshape(NO * V, K * V)
    right_side = jnp.transpose(sym_ints, (0, 3, 1, 2)).reshape(K * V, NO * V)
    product = jnp.dot(left_side, right_side, preferred_element_type=jnp.float32).reshape(NO, V, NO, V)
    return jnp.transpose(product, (0, 2, 3, 1)) + jnp.transpose(product, (2, 0, 1, 3))
```

```python
import jax
import jax.numpy as jnp
from jax import lax
from jax.experimental import pallas as pl
from jax.experimental.pallas import tpu as pltpu
from jax.sharding import PartitionSpec as P

NX = NY = NZ = 4
NJ = 16
NS = 8
TILE = 64
V = 512
N_SEMS = 96
BF16 = jnp.bfloat16
F32 = jnp.float32


def wrap(at, step, size):
    return lax.rem(at + step + size, size)


def kernel(
    amps_hbm, ints_hbm, occ_ref, slab_ref, virt_ref, out_ref,
    amps, ints, row_labels, to_sibling, from_sibling, part, from_ring,
    pair_w, pair_a, slab_w, slab_a, load_sems, send_sems, recv_sems,
):
    pair, slab = lax.axis_index("pair"), lax.axis_index("slab")
    z, x = pair // NX, lax.rem(pair, NX)
    y, core = slab // 2, lax.rem(slab, 2)
    sibling_core = 1 - core

    def at_pair(dz, dx):
        return wrap(z, dz, NZ) * NX + wrap(x, dx, NX)

    def at_slab(dy, own_core=True):
        return wrap(y, dy, NY) * 2 + (core if own_core else sibling_core)

    device = {
        "x+": (at_pair(0, 1), slab), "x-": (at_pair(0, -1), slab),
        "z+": (at_pair(1, 0), slab), "z-": (at_pair(-1, 0), slab),
        "y+": (pair, at_slab(1)), "y-": (pair, at_slab(-1)),
        "sibling": (pair, at_slab(0, False)),
    }

    load_amps = pltpu.make_async_copy(amps_hbm.at[0, 0], amps, load_sems.at[0])
    load_ints = pltpu.make_async_copy(ints_hbm.at[:, 0], ints, load_sems.at[1])
    load_amps.start()
    load_ints.start()

    barrier = pltpu.get_barrier_semaphore()
    for to in device.values():
        pl.semaphore_signal(barrier, inc=1, device_id=to, device_id_type=pl.DeviceIdType.MESH)

    started, order = [], {}

    def copy(name, src, dst, to):
        at = order.setdefault(name, len(order))
        return pltpu.make_async_remote_copy(
            src_ref=src, dst_ref=dst, send_sem=send_sems.at[at], recv_sem=recv_sems.at[at],
            device_id=device[to], device_id_type=pl.DeviceIdType.MESH,
        )

    def send(name, src, dst, to):
        sent = copy(name, src, dst, to)
        sent.start()
        started.append(sent)

    def arrive(name, dst, to):
        copy(name, dst, dst, to).wait_recv()

    columns = virt_ref[...]
    for at in range(V // 128):
        lanes = jnp.broadcast_to(columns[:, at * 128 : (at + 1) * 128], (128, 128))
        row_labels[at * 128 : (at + 1) * 128, :] = lanes.T

    def pair_labels(tile):
        rows = row_labels[pl.ds(pl.multiple_of(tile * TILE, TILE), TILE), :]
        return jnp.concatenate([rows] * (V // 128), axis=1) ^ columns

    own_label = occ_ref[pair]
    amps_label = own_label ^ slab_ref[slab]

    def masked(tile):
        block = amps[pl.ds(pl.multiple_of(tile * TILE, TILE), TILE), :].astype(F32)
        chosen = jnp.where(pair_labels(tile) == amps_label, block, 0.0)
        return chosen.astype(BF16).reshape(2, 2, 16, V)

    load_amps.wait()
    for at in range(NY):
        to_sibling[at] = masked(2 * at + sibling_core)

    pl.semaphore_wait(barrier, len(device))
    send("merge", to_sibling, from_sibling, "sibling")

    load_ints.wait()
    wanted = pair_labels(slab) ^ own_label
    w = jnp.zeros((TILE, V), F32)
    for k in range(8):
        w = jnp.where(wanted == slab_ref[k], ints[k].astype(F32), w)
    w = w.astype(BF16).reshape(2, 2, 16, V)
    pair_w[pair] = w
    slab_w[slab] = w

    def pair_start(tag, buf):
        for to in ("x+", "x-", "z+", "z-"):
            send(tag + to, buf.at[pair], buf.at[pair], to)

    def pair_near(tag, buf):
        for axis, other, half in (("x", "z", 0), ("z", "x", 1)):
            for came, step, on, quarter in (("-", -1, "+", 0), ("+", 1, "-", 1)):
                at = at_pair(0, step) if axis == "x" else at_pair(step, 0)
                arrive(tag + axis + on, buf.at[at], axis + on)
                send(tag + "far" + axis + on, buf.at[at, :, quarter], buf.at[at, :, quarter], axis + on)
                for way in ("+", "-"):
                    send(tag + "turn" + axis + came + other + way, buf.at[at, half], buf.at[at, half], other + way)

    def pair_middle(tag, buf):
        for axis, other, half in (("x", "z", 0), ("z", "x", 1)):
            at = at_pair(0, 2) if axis == "x" else at_pair(2, 0)
            for on, quarter in (("+", 0), ("-", 1)):
                arrive(tag + "far" + axis + on, buf.at[at, :, quarter], axis + on)
            for way in ("+", "-"):
                send(tag + "turn" + axis + "2" + other + way, buf.at[at, half], buf.at[at, half], other + way)
        for axis, other, half in (("x", "z", 0), ("z", "x", 1)):
            for turn, side in (("-", -1), ("+", 1)):
                for step, way, quarter in ((-1, "+", 0), (1, "-", 1)):
                    at = at_pair(step, side) if axis == "x" else at_pair(side, step)
                    arrive(tag + "turn" + axis + turn + other + way, buf.at[at, half], other + way)
                    piece = buf.at[at, half, quarter]
                    send(tag + "last" + axis + turn + other + way, piece, piece, other + way)

    def pair_far(tag, buf):
        for axis, other, half in (("x", "z", 0), ("z", "x", 1)):
            for step, way, quarter in ((-1, "+", 0), (1, "-", 1)):
                at = at_pair(step, 2) if axis == "x" else at_pair(2, step)
                arrive(tag + "turn" + axis + "2" + other + way, buf.at[at, half], other + way)
                piece = buf.at[at, half, quarter]
                send(tag + "last" + axis + "2" + other + way, piece, piece, other + way)
        for axis, other, half in (("x", "z", 0), ("z", "x", 1)):
            for turn, side in (("-", -1), ("+", 1)):
                at = at_pair(2, side) if axis == "x" else at_pair(side, 2)
                for way, quarter in (("+", 0), ("-", 1)):
                    arrive(tag + "last" + axis + turn + other + way, buf.at[at, half, quarter], other + way)

    def pair_end(tag, buf):
        at = at_pair(2, 2)
        for axis, other, half in (("x", "z", 0), ("z", "x", 1)):
            for way, quarter in (("+", 0), ("-", 1)):
                arrive(tag + "last" + axis + "2" + other + way, buf.at[at, half, quarter], other + way)

    def slab_start(tag, buf):
        for to in ("y+", "y-", "sibling"):
            send(tag + to, buf.at[slab], buf.at[slab], to)

    def slab_near(tag, buf):
        for step, on, half in ((-1, "+", 0), (1, "-", 1)):
            at = at_slab(step)
            arrive(tag + "y" + on, buf.at[at], "y" + on)
            send(tag + "far" + on, buf.at[at, half], buf.at[at, half], "y" + on)
            send(tag + "over" + on, buf.at[at], buf.at[at], "sibling")

    def slab_far(tag, buf):
        at = at_slab(2)
        for on, half in (("+", 0), ("-", 1)):
            arrive(tag + "far" + on, buf.at[at, half], "y" + on)
        send(tag + "over2", buf.at[at], buf.at[at], "sibling")

    def slab_end(tag, buf):
        arrive(tag + "sibling", buf.at[at_slab(0, False)], "sibling")
        arrive(tag + "over+", buf.at[at_slab(-1, False)], "sibling")
        arrive(tag + "over-", buf.at[at_slab(1, False)], "sibling")
        arrive(tag + "over2", buf.at[at_slab(2, False)], "sibling")

    pair_start("pw", pair_w)
    slab_start("sw", slab_w)

    for at in range(NY):
        part[at] = masked(2 * at + core)
    arrive("merge", from_sibling, "sibling")
    part[...] = part[...] + from_sibling[...]

    up, down, across = wrap(y, 1, NY), wrap(y, -1, NY), wrap(y, 2, NY)
    send("ring far+", part.at[across, 0], from_ring.at[0], "y+")
    send("ring far-", part.at[across, 1], from_ring.at[1], "y-")
    send("ring now+", part.at[up, 1], from_ring.at[2], "y+")
    send("ring now-", part.at[down, 0], from_ring.at[3], "y-")

    pair_near("pw", pair_w)

    arrive("ring far+", from_ring.at[0], "y+")
    part[up, 0] = part[up, 0] + from_ring[0]
    send("ring late+", part.at[up, 0], from_ring.at[4], "y+")
    arrive("ring far-", from_ring.at[1], "y-")
    part[down, 1] = part[down, 1] + from_ring[1]
    send("ring late-", part.at[down, 1], from_ring.at[5], "y-")

    slab_near("sw", slab_w)
    pair_middle("pw", pair_w)

    arrive("ring now+", from_ring.at[2], "y+")
    arrive("ring now-", from_ring.at[3], "y-")
    arrive("ring late+", from_ring.at[4], "y+")
    arrive("ring late-", from_ring.at[5], "y-")
    first = part[y, 0] + from_ring[3] + from_ring[4]
    second = part[y, 1] + from_ring[2] + from_ring[5]
    for half, value in ((0, first), (1, second)):
        pair_a[pair, half] = value
        slab_a[slab, half] = value
    slab_start("sa", slab_a)
    pair_start("pa", pair_a)

    slab_far("sw", slab_w)
    pair_far("pw", pair_w)
    slab_near("sa", slab_a)
    pair_near("pa", pair_a)
    slab_end("sw", slab_w)
    pair_end("pw", pair_w)
    slab_far("sa", slab_a)
    pair_middle("pa", pair_a)
    slab_end("sa", slab_a)

    def times(rows, every):
        return lax.dot_general(rows, every, (((1,), (1,)), ((), ())), preferred_element_type=F32)

    def first_term(at, n):
        every_a = slab_a[...].reshape(V, V)
        rows = pair_w[pl.ds(at, n)].reshape(n * TILE, V)
        out_ref[0, pl.ds(at, n)] = times(rows, every_a).reshape(n, TILE, V)

    def second_term(j):
        every_w = slab_w[...].reshape(V, V)
        term = times(pair_a[j].reshape(TILE, V), every_w)
        kept = pair_labels(slab) == (own_label ^ occ_ref[j])
        out_ref[0, j] = jnp.where(kept, out_ref[0, j] + term, 0.0)

    @pl.loop(0, NJ // 4)
    def _(at):
        first_term(at * 4, 4)

    pair_far("pa", pair_a)
    pair_end("pa", pair_a)

    @pl.loop(0, NJ)
    def _(j):
        second_term(j)

    for sent in started:
        sent.wait_send()


def solution(mesh):
    placed = (P("pair", "slab", None, None), P(None, "pair", "slab", None), P(), P(), P())
    piece = (2, 2, 16, V)

    def local(amplitudes, integrals, occ_irrep, slab_irrep, virt_irrep):
        vmem = pl.BlockSpec(memory_space=pltpu.VMEM)
        smem = pl.BlockSpec(memory_space=pltpu.SMEM)
        anywhere = pl.BlockSpec(memory_space=pl.ANY)
        return pl.pallas_call(
            kernel,
            out_shape=jax.ShapeDtypeStruct((1, NJ, TILE, V), F32),
            in_specs=[anywhere, anywhere, smem, smem, vmem],
            out_specs=vmem,
            scratch_shapes=[
                pltpu.VMEM((V, V), BF16),
                pltpu.VMEM((8, TILE, V), BF16),
                pltpu.VMEM((V, 128), jnp.int32),
                pltpu.VMEM((NY, *piece), BF16),
                pltpu.VMEM((NY, *piece), BF16),
                pltpu.VMEM((NY, *piece), BF16),
                pltpu.VMEM((6, 2, 16, V), BF16),
                pltpu.VMEM((NJ, *piece), BF16),
                pltpu.VMEM((NJ, *piece), BF16),
                pltpu.VMEM((NS, *piece), BF16),
                pltpu.VMEM((NS, *piece), BF16),
                pltpu.SemaphoreType.DMA((2,)),
                pltpu.SemaphoreType.DMA((N_SEMS,)),
                pltpu.SemaphoreType.DMA((N_SEMS,)),
            ],
            compiler_params=pltpu.CompilerParams(
                collective_id=0, has_side_effects=True, vmem_limit_bytes=32 * 1024 * 1024
            ),
        )(amplitudes, integrals, occ_irrep.reshape(NJ), slab_irrep, virt_irrep.reshape(1, V))

    return jax.shard_map(
        local, mesh=mesh, in_specs=placed, out_specs=P("pair", None, "slab", None), check_vma=False
    )
```

```python
import jax
import jax.numpy as jnp
from jax import lax
from jax.experimental import pallas as pl
from jax.experimental.pallas import tpu as pltpu
from jax.sharding import PartitionSpec as P

NX = NY = NZ = 4
NJ = 16
NS = 8
TILE = 64
V = 512
N_SEMS = 66
STEPS = (1, -1, 2)
BF16 = jnp.bfloat16
F32 = jnp.float32


def wrap(at, step, size):
    return lax.rem(at + step + size, size)


def kernel(
    amps_hbm, ints_hbm, occ_hbm, slab_hbm, virt_hbm, out_ref,
    amps, ints, occ_ref, slab_ref, virt_ref, row_labels, to_sibling, from_sibling, part, from_ring,
    pair_w, pair_a, slab_w, slab_a, load_sems, send_sems, recv_sems,
):
    pair, slab = lax.axis_index("pair"), lax.axis_index("slab")
    z, x = pair // NX, lax.rem(pair, NX)
    y, core = slab // 2, lax.rem(slab, 2)
    sibling_core = 1 - core

    def at_pair(dz, dx):
        return wrap(z, dz, NZ) * NX + wrap(x, dx, NX)

    def at_slab(dy, own_core=True):
        return wrap(y, dy, NY) * 2 + (core if own_core else sibling_core)

    device = {"sibling": (pair, at_slab(0, False))}
    for step in STEPS:
        device["x", step] = (at_pair(0, step), slab)
        device["z", step] = (at_pair(step, 0), slab)
        device["y", step] = (pair, at_slab(step))

    loads = [
        pltpu.make_async_copy(src, dst, load_sems.at[at])
        for at, (src, dst) in enumerate((
            (virt_hbm, virt_ref),
            (occ_hbm, occ_ref),
            (slab_hbm, slab_ref),
            (amps_hbm.at[:, sibling_core], amps.at[sibling_core]),
            (ints_hbm.at[:, 0], ints),
            (amps_hbm.at[:, core], amps.at[core]),
        ))
    ]
    for load in loads:
        load.start()

    barrier = pltpu.get_barrier_semaphore()
    for to in device.values():
        pl.semaphore_signal(barrier, inc=1, device_id=to, device_id_type=pl.DeviceIdType.MESH)

    started, order = [], {}

    def copy(name, src, dst, to):
        at = order.setdefault((name, to), len(order))
        return pltpu.make_async_remote_copy(
            src_ref=src, dst_ref=dst, send_sem=send_sems.at[at], recv_sem=recv_sems.at[at],
            device_id=device[to], device_id_type=pl.DeviceIdType.MESH,
        )

    def send(name, src, dst, to):
        sent = copy(name, src, dst, to)
        sent.start()
        started.append(sent)

    def arrive(name, dst, to):
        copy(name, dst, dst, to).wait_recv()

    for load in loads[:3]:
        load.wait()
    columns = virt_ref[...]
    for at in range(V // 128):
        lanes = jnp.broadcast_to(columns[:, at * 128 : (at + 1) * 128], (128, 128))
        row_labels[at * 128 : (at + 1) * 128, :] = lanes.T

    def pair_labels(tile):
        rows = row_labels[pl.ds(pl.multiple_of(tile * TILE, TILE), TILE), :]
        return jnp.concatenate([rows] * (V // 128), axis=1) ^ columns

    own_label = occ_ref[pair]
    amps_label = own_label ^ slab_ref[slab]

    def masked(at, of_core):
        block = amps[of_core, at].astype(F32)
        chosen = jnp.where(pair_labels(2 * at + of_core) == amps_label, block, 0.0)
        return chosen.astype(BF16).reshape(2, 2, 16, V)

    loads[3].wait()
    for at in range(NY):
        to_sibling[at] = masked(at, sibling_core)

    loads[4].wait()
    wanted = pair_labels(slab) ^ own_label
    w = jnp.zeros((TILE, V), F32)
    for k in range(8):
        w = jnp.where(wanted == slab_ref[k], ints[k].astype(F32), w)
    w = w.astype(BF16).reshape(2, 2, 16, V)
    pair_w[pair] = w
    slab_w[slab] = w

    axes = (("x", "z", 0), ("z", "x", 1))

    def beside(axis, step, other=0):
        return at_pair(other, step) if axis == "x" else at_pair(step, other)

    def pair_start(tag, buf):
        for step in STEPS:
            for axis in ("x", "z"):
                send(tag, buf.at[pair], buf.at[pair], (axis, step))

    def pair_turn(tag, buf):
        for step in STEPS:
            for axis, other, half in axes:
                at = beside(axis, -step)
                arrive(tag, buf.at[at], (axis, step))
                for way in STEPS:
                    send((tag, step), buf.at[at, half], buf.at[at, half], (other, way))

    def pair_end(tag, buf, step):
        for way in STEPS:
            for axis, other, half in axes:
                at = beside(axis, -step, -way) if axis == "x" else beside(axis, -way, -step)
                turned = step if axis == "x" else way
                sent = way if axis == "x" else step
                arrive((tag, turned), buf.at[at, half], (other, sent))

    def slab_start(tag, buf):
        for to in (("y", 1), ("y", -1), ("y", 2), "sibling"):
            send(tag, buf.at[slab], buf.at[slab], to)

    def slab_over(tag, buf):
        for step in STEPS:
            at = at_slab(-step)
            arrive(tag, buf.at[at], ("y", step))
            send((tag, step), buf.at[at], buf.at[at], "sibling")

    def slab_end(tag, buf):
        arrive(tag, buf.at[at_slab(0, False)], "sibling")
        for step in STEPS:
            arrive((tag, step), buf.at[at_slab(-step, False)], "sibling")

    pl.semaphore_wait(barrier, len(device))
    send("merge", to_sibling, from_sibling, "sibling")
    pair_start("pw", pair_w)
    slab_start("sw", slab_w)

    loads[5].wait()
    for at in range(NY):
        part[at] = masked(at, core)
    arrive("merge", from_sibling, "sibling")
    part[...] = part[...] + from_sibling[...]
    for at, step in enumerate(STEPS):
        send("ring", part.at[wrap(y, step, NY)], from_ring.at[at], ("y", step))

    pair_turn("pw", pair_w)
    slab_over("sw", slab_w)

    total = part[y]
    for at, step in enumerate(STEPS):
        arrive("ring", from_ring.at[at], ("y", step))
        total = total + from_ring[at]
    pair_a[pair] = total
    slab_a[slab] = total
    pair_start("pa", pair_a)
    slab_start("sa", slab_a)

    pair_turn("pa", pair_a)
    slab_over("sa", slab_a)
    for step in STEPS:
        pair_end("pw", pair_w, step)
    slab_end("sw", slab_w)
    slab_end("sa", slab_a)

    def times(rows, every):
        return lax.dot_general(rows, every, (((1,), (1,)), ((), ())), preferred_element_type=F32)

    @pl.loop(0, 2)
    def _(at):
        half = NJ // 2
        rows = pair_w[pl.ds(at * half, half)].reshape(half * TILE, V)
        out_ref[0, pl.ds(at * half, half)] = times(rows, slab_a[...].reshape(V, V)).reshape(half, TILE, V)

    labels = pair_labels(slab) ^ own_label

    def second_term(group):
        rows = jnp.concatenate([pair_a[j].reshape(TILE, V) for j in group], axis=0)
        term = times(rows, slab_w[...].reshape(V, V))
        for at, j in enumerate(group):
            both = out_ref[0, j] + term[at * TILE : (at + 1) * TILE]
            out_ref[0, j] = jnp.where(labels == occ_ref[j], both, 0.0)

    second_term([pair] + [beside(axis, step) for axis in ("x", "z") for step in STEPS])
    for step in STEPS:
        pair_end("pa", pair_a, step)
        second_term([beside("x", -step, -way) for way in STEPS])

    assert len(order) == N_SEMS
    for sent in started:
        sent.wait_send()


def solution(mesh):
    placed = (P("pair", "slab", None, None), P(None, "pair", "slab", None), P(), P(), P())
    piece = (2, 2, 16, V)

    def local(amplitudes, integrals, occ_irrep, slab_irrep, virt_irrep):
        operands = (
            amplitudes.reshape(NY, 2, TILE, V), integrals, occ_irrep.reshape(NJ), slab_irrep, virt_irrep.reshape(1, V)
        )
        return pl.pallas_call(
            kernel,
            out_shape=jax.ShapeDtypeStruct((1, NJ, TILE, V), F32),
            in_specs=[pl.BlockSpec(memory_space=pltpu.HBM)] * 5,
            out_specs=pl.BlockSpec(memory_space=pltpu.VMEM),
            scratch_shapes=[
                pltpu.VMEM((2, NY, TILE, V), BF16),
                pltpu.VMEM((8, TILE, V), BF16),
                pltpu.SMEM((NJ,), jnp.int32),
                pltpu.SMEM((8,), jnp.int32),
                pltpu.VMEM((1, V), jnp.int32),
                pltpu.VMEM((V, 128), jnp.int32),
                pltpu.VMEM((NY, *piece), BF16),
                pltpu.VMEM((NY, *piece), BF16),
                pltpu.VMEM((NY, *piece), BF16),
                pltpu.VMEM((3, *piece), BF16),
                pltpu.VMEM((NJ, *piece), BF16),
                pltpu.VMEM((NJ, *piece), BF16),
                pltpu.VMEM((NS, *piece), BF16),
                pltpu.VMEM((NS, *piece), BF16),
                pltpu.SemaphoreType.DMA((6,)),
                pltpu.SemaphoreType.DMA((N_SEMS,)),
                pltpu.SemaphoreType.DMA((N_SEMS,)),
            ],
            compiler_params=pltpu.CompilerParams(
                collective_id=0, has_side_effects=True, vmem_limit_bytes=32 * 1024 * 1024
            ),
        )(*(pltpu.with_memory_space_constraint(operand, pltpu.HBM) for operand in operands))

    return jax.shard_map(
        local, mesh=mesh, in_specs=placed, out_specs=P("pair", None, "slab", None), check_vma=False
    )
```

```python
import jax
import jax.numpy as jnp
from jax import lax
from jax.experimental import pallas as pl
from jax.experimental.pallas import tpu as pltpu
from jax.sharding import PartitionSpec as P

NX = NY = NZ = 4
NJ = 16
NS = 8
TILE = 64
V = 512
N_SEMS = 37
N_SENT = 204
STEPS = (1, -1, 2)
BF16 = jnp.bfloat16
F32 = jnp.float32


def wrap(at, step, size):
    return lax.rem(at + step + size, size)


def kernel(
    amps_hbm, ints_hbm, occ_hbm, slab_hbm, virt_hbm, out_ref,
    amps, ints, occ_ref, slab_ref, virt_ref, row_labels, from_sibling, part, from_ring,
    pair_w, pair_a, slab_w, slab_a, spent, load_sems, send_sems, recv_sems,
):
    pair, slab = lax.axis_index("pair"), lax.axis_index("slab")
    z, x = pair // NX, lax.rem(pair, NX)
    y, core = slab // 2, lax.rem(slab, 2)
    sibling_core = 1 - core

    def at_pair(dz, dx):
        return wrap(z, dz, NZ) * NX + wrap(x, dx, NX)

    def at_slab(dy, own_core=True):
        return wrap(y, dy, NY) * 2 + (core if own_core else sibling_core)

    device = {"sibling": (pair, at_slab(0, False))}
    for step in STEPS:
        device["x", step] = (at_pair(0, step), slab)
        device["z", step] = (at_pair(step, 0), slab)
        device["y", step] = (pair, at_slab(step))

    loads = [
        pltpu.make_async_copy(src, dst, load_sems.at[at])
        for at, (src, dst) in enumerate((
            (virt_hbm, virt_ref),
            (occ_hbm, occ_ref),
            (slab_hbm, slab_ref),
            (amps_hbm.at[:, core], amps),
            (ints_hbm.at[:, 0], ints),
        ))
    ]
    for load in loads:
        load.start()

    barrier = pltpu.get_barrier_semaphore()
    for to in device.values():
        pl.semaphore_signal(barrier, inc=1, device_id=to, device_id_type=pl.DeviceIdType.MESH)

    order, sent = {}, []

    def copy(group, src, dst, to):
        at = order.setdefault(group, len(order))
        return pltpu.make_async_remote_copy(
            src_ref=src, dst_ref=dst, send_sem=send_sems.at[0], recv_sem=recv_sems.at[at],
            device_id=device[to], device_id_type=pl.DeviceIdType.MESH,
        )

    def send(group, src, dst, to):
        copy(group, src, dst, to).start()
        sent.append(src.size // (16 * V))

    def arrive(group, like):
        copy(group, like, like, "sibling").wait_recv()

    pl.semaphore_wait(barrier, len(device))
    send("merge", amps_hbm.at[:, sibling_core], from_sibling, "sibling")

    for load in loads[:3]:
        load.wait()
    columns = virt_ref[...]
    for at in range(V // 128):
        lanes = jnp.broadcast_to(columns[:, at * 128 : (at + 1) * 128], (128, 128))
        row_labels[at * 128 : (at + 1) * 128, :] = lanes.T

    def pair_labels(tile):
        rows = row_labels[pl.ds(pl.multiple_of(tile * TILE, TILE), TILE), :]
        return jnp.concatenate([rows] * (V // 128), axis=1) ^ columns

    own_label = occ_ref[pair]
    amps_label = own_label ^ slab_ref[slab]
    sibling_label = own_label ^ slab_ref[at_slab(0, False)]

    loads[4].wait()
    wanted = pair_labels(slab) ^ own_label
    w = jnp.zeros((TILE, V), F32)
    for k in range(8):
        w = jnp.where(wanted == slab_ref[k], ints[k].astype(F32), w)
    w = w.astype(BF16).reshape(2, 2, 16, V)
    pair_w[pair] = w
    slab_w[slab] = w

    axes = (("x", "z", 0), ("z", "x", 1))

    def beside(axis, step, other=0):
        return at_pair(other, step) if axis == "x" else at_pair(step, other)

    def pair_start(tag, buf, chunk):
        for step in STEPS:
            for axis, _, half in axes:
                own = buf.at[pair, half, chunk]
                send((tag, str(chunk), axis, step), own, own, (axis, step))
        for step in STEPS:
            for axis, _, half in axes:
                own = buf.at[pair, 1 - half, chunk]
                send((tag, "own"), own, own, (axis, step))

    def pair_turn(tag, buf, chunk):
        for step in STEPS:
            for axis, other, half in axes:
                piece = buf.at[beside(axis, -step), half, chunk]
                arrive((tag, str(chunk), axis, step), piece)
                for way in STEPS:
                    send((tag, "turned", step if axis == "x" else way), piece, piece, (other, way))

    def pair_near(tag, buf):
        arrive((tag, "own"), buf.at[pl.ds(0, 3)])

    def pair_end(tag, buf, step):
        arrive((tag, "turned", step), buf.at[pl.ds(0, 3)])

    def slab_start(tag, buf):
        for step in STEPS:
            send((tag, step), buf.at[slab], buf.at[slab], ("y", step))
        send((tag, "sibling"), buf.at[slab], buf.at[slab], "sibling")

    def slab_over(tag, buf):
        for step in STEPS:
            piece = buf.at[at_slab(-step)]
            arrive((tag, step), piece)
            send((tag, "sibling"), piece, piece, "sibling")

    def slab_end(tag, buf):
        arrive((tag, "sibling"), buf.at[pl.ds(0, NY)])

    whole = pl.ds(0, 2)
    pair_start("pw", pair_w, whole)

    loads[3].wait()
    arrive("merge", from_sibling)
    for at in range(NY):
        labels = pair_labels(2 * at + core)
        other = jnp.where(labels == sibling_label, from_sibling[at].astype(F32), 0.0)
        part[at] = jnp.where(labels == amps_label, amps[at].astype(F32), other).astype(BF16).reshape(2, 2, 16, V)
    for chunk in range(2):
        for at, step in enumerate(STEPS):
            send(("ring", chunk), part.at[wrap(y, step, NY), :, chunk], from_ring.at[at, :, chunk], ("y", step))
    slab_start("sw", slab_w)

    def ring_end(chunk):
        arrive(("ring", chunk), from_ring.at[:, :, chunk])
        total = part[y, :, chunk]
        for at in range(len(STEPS)):
            total = total + from_ring[at, :, chunk]
        pair_a[pair, :, chunk] = total
        slab_a[slab, :, chunk] = total

    pair_turn("pw", pair_w, whole)
    for chunk in range(2):
        ring_end(chunk)
        pair_start("pa", pair_a, chunk)
    slab_start("sa", slab_a)
    slab_over("sw", slab_w)
    for chunk in range(2):
        pair_turn("pa", pair_a, chunk)
    slab_over("sa", slab_a)
    pair_near("pw", pair_w)
    for step in STEPS:
        pair_end("pw", pair_w, step)
    slab_end("sw", slab_w)
    slab_end("sa", slab_a)

    def times(rows, every):
        return lax.dot_general(rows, every, (((1,), (1,)), ((), ())), preferred_element_type=F32)

    @pl.loop(0, 2)
    def _(at):
        half = NJ // 2
        rows = pair_w[pl.ds(at * half, half)].reshape(half * TILE, V)
        out_ref[0, pl.ds(at * half, half)] = times(rows, slab_a[...].reshape(V, V)).reshape(half, TILE, V)

    labels = pair_labels(slab) ^ own_label

    def second_term(group):
        rows = jnp.concatenate([pair_a[j].reshape(TILE, V) for j in group], axis=0)
        term = times(rows, slab_w[...].reshape(V, V))
        for at, j in enumerate(group):
            both = out_ref[0, j] + term[at * TILE : (at + 1) * TILE]
            out_ref[0, j] = jnp.where(labels == occ_ref[j], both, 0.0)

    pair_near("pa", pair_a)
    second_term([pair] + [beside(axis, step) for axis in ("x", "z") for step in STEPS])
    for step in STEPS:
        pair_end("pa", pair_a, step)
        second_term([beside("x", -step, -way) for way in STEPS])

    assert len(order) == N_SEMS
    assert sum(sent) == N_SENT
    copy("merge", spent, spent, "sibling").wait_send()


def solution(mesh):
    placed = (P("pair", "slab", None, None), P(None, "pair", "slab", None), P(), P(), P())
    piece = (2, 2, 16, V)

    def local(amplitudes, integrals, occ_irrep, slab_irrep, virt_irrep):
        operands = (
            amplitudes.reshape(NY, 2, TILE, V), integrals, occ_irrep.reshape(NJ), slab_irrep, virt_irrep.reshape(1, V)
        )
        return pl.pallas_call(
            kernel,
            out_shape=jax.ShapeDtypeStruct((1, NJ, TILE, V), F32),
            in_specs=[pl.BlockSpec(memory_space=pltpu.HBM)] * 5,
            out_specs=pl.BlockSpec(memory_space=pltpu.VMEM),
            scratch_shapes=[
                pltpu.VMEM((NY, TILE, V), BF16),
                pltpu.VMEM((8, TILE, V), BF16),
                pltpu.SMEM((NJ,), jnp.int32),
                pltpu.SMEM((8,), jnp.int32),
                pltpu.VMEM((1, V), jnp.int32),
                pltpu.VMEM((V, 128), jnp.int32),
                pltpu.VMEM((NY, TILE, V), BF16),
                pltpu.VMEM((NY, *piece), BF16),
                pltpu.VMEM((3, *piece), BF16),
                pltpu.VMEM((NJ, *piece), BF16),
                pltpu.VMEM((NJ, *piece), BF16),
                pltpu.VMEM((NS, *piece), BF16),
                pltpu.VMEM((NS, *piece), BF16),
                pltpu.VMEM((N_SENT, 16, V), BF16),
                pltpu.SemaphoreType.DMA((5,)),
                pltpu.SemaphoreType.DMA((1,)),
                pltpu.SemaphoreType.DMA((N_SEMS,)),
            ],
            compiler_params=pltpu.CompilerParams(
                collective_id=0, has_side_effects=True, vmem_limit_bytes=32 * 1024 * 1024
            ),
        )(*(pltpu.with_memory_space_constraint(operand, pltpu.HBM) for operand in operands))

    return jax.shard_map(
        local, mesh=mesh, in_specs=placed, out_specs=P("pair", None, "slab", None), check_vma=False
    )
```

```python
import jax
import jax.numpy as jnp
from jax import lax
from jax.experimental import pallas as pl
from jax.experimental.pallas import tpu as pltpu
from jax.sharding import PartitionSpec as P

NX = NY = NZ = 4
NJ = 16
NS = 8
TILE = 64
V = 512
N_SEMS = 35
N_SENT = 204
NEAR = (1, -1)
STEPS = (1, -1, 2)
BF16 = jnp.bfloat16
F32 = jnp.float32


def wrap(at, step, size):
    return lax.rem(at + step + size, size)


def kernel(
    amps_hbm, ints_hbm, occ_hbm, slab_hbm, virt_hbm, out_ref,
    amps, ints, occ_ref, slab_ref, virt_ref, row_labels, from_sibling, part, from_ring,
    pair_w, pair_a, slab_w, slab_a, spent, load_sems, send_sems, recv_sems,
):
    pair, slab = lax.axis_index("pair"), lax.axis_index("slab")
    z, x = pair // NX, lax.rem(pair, NX)
    y, core = slab // 2, lax.rem(slab, 2)
    sibling_core = 1 - core

    def at_pair(dz, dx):
        return wrap(z, dz, NZ) * NX + wrap(x, dx, NX)

    def at_slab(dy, own_core=True):
        return wrap(y, dy, NY) * 2 + (core if own_core else sibling_core)

    device = {"sibling": (pair, at_slab(0, False))}
    for step in STEPS:
        device["x", step] = (at_pair(0, step), slab)
        device["z", step] = (at_pair(step, 0), slab)
        device["y", step] = (pair, at_slab(step))

    loads = [
        pltpu.make_async_copy(src, dst, load_sems.at[at])
        for at, (src, dst) in enumerate((
            (virt_hbm, virt_ref),
            (occ_hbm, occ_ref),
            (slab_hbm, slab_ref),
            (amps_hbm.at[:, core], amps),
            (ints_hbm.at[:, 0], ints),
        ))
    ]
    for load in loads:
        load.start()

    barrier = pltpu.get_barrier_semaphore()
    for to in device.values():
        pl.semaphore_signal(barrier, inc=1, device_id=to, device_id_type=pl.DeviceIdType.MESH)

    order, sent = {}, []

    def copy(group, src, dst, to):
        at = order.setdefault(group, len(order))
        return pltpu.make_async_remote_copy(
            src_ref=src, dst_ref=dst, send_sem=send_sems.at[0], recv_sem=recv_sems.at[at],
            device_id=device[to], device_id_type=pl.DeviceIdType.MESH,
        )

    def send(group, src, dst, to):
        copy(group, src, dst, to).start()
        sent.append(src.size // (16 * V))

    def arrive(group, like):
        copy(group, like, like, "sibling").wait_recv()

    pl.semaphore_wait(barrier, len(device))
    send("merge", amps_hbm.at[:, sibling_core], from_sibling, "sibling")

    for load in loads[:3]:
        load.wait()
    columns = virt_ref[...]
    for at in range(V // 128):
        lanes = jnp.broadcast_to(columns[:, at * 128 : (at + 1) * 128], (128, 128))
        row_labels[at * 128 : (at + 1) * 128, :] = lanes.T

    def pair_labels(tile):
        rows = row_labels[pl.ds(pl.multiple_of(tile * TILE, TILE), TILE), :]
        return jnp.concatenate([rows] * (V // 128), axis=1) ^ columns

    own_label = occ_ref[pair]
    amps_label = own_label ^ slab_ref[slab]
    sibling_label = own_label ^ slab_ref[at_slab(0, False)]

    loads[4].wait()
    wanted = pair_labels(slab) ^ own_label
    w = jnp.zeros((TILE, V), F32)
    for k in range(8):
        w = jnp.where(wanted == slab_ref[k], ints[k].astype(F32), w)
    w = w.astype(BF16).reshape(2, 2, 16, V)
    pair_w[pair] = w
    slab_w[slab] = w

    axes = (("x", "z", 0), ("z", "x", 1))

    def beside(axis, step, other=0):
        return at_pair(other, step) if axis == "x" else at_pair(step, other)

    def pair_start(tag, buf, chunk):
        for axis, _, _ in axes:
            own = buf.at[pair, :, chunk]
            send((tag, str(chunk), axis, 2), own, own, (axis, 2))
        for step in NEAR:
            for axis, _, half in axes:
                own = buf.at[pair, half, chunk]
                send((tag, str(chunk), axis, step), own, own, (axis, step))
        for step in NEAR:
            for axis, _, half in axes:
                own = buf.at[pair, 1 - half, chunk]
                send((tag, "own"), own, own, (axis, step))

    def pair_turn(tag, buf, chunk):
        for step in NEAR:
            for axis, other, half in axes:
                piece = buf.at[beside(axis, -step), half, chunk]
                arrive((tag, str(chunk), axis, step), piece)
                for way in NEAR:
                    send((tag, "near"), piece, piece, (other, way))
        for axis, other, half in axes:
            piece = buf.at[beside(axis, 2), :, chunk]
            arrive((tag, str(chunk), axis, 2), piece)
            for way in NEAR:
                send((tag, "far"), piece, piece, (other, way))
            piece = buf.at[beside(axis, 2), half, chunk]
            send((tag, "far"), piece, piece, (other, 2))

    def pair_own(tag, buf):
        arrive((tag, "own"), buf.at[pl.ds(0, 2)])

    def pair_near(tag, buf):
        arrive((tag, "near"), buf.at[pl.ds(0, 4)])

    def pair_far(tag, buf):
        arrive((tag, "far"), buf.at[pl.ds(0, 5)])

    def slab_start(tag, buf, steps):
        for step in steps:
            send((tag, step), buf.at[slab], buf.at[slab], ("y", step))

    def slab_over(tag, buf):
        send((tag, "sibling"), buf.at[slab], buf.at[slab], "sibling")
        for step in STEPS:
            piece = buf.at[at_slab(-step)]
            arrive((tag, step), piece)
            send((tag, "sibling"), piece, piece, "sibling")

    def slab_end(tag, buf):
        arrive((tag, "sibling"), buf.at[pl.ds(0, NY)])

    whole = pl.ds(0, 2)
    pair_start("pw", pair_w, whole)
    slab_start("sw", slab_w, NEAR)

    loads[3].wait()
    arrive("merge", from_sibling)
    for at in range(NY):
        labels = pair_labels(2 * at + core)
        other = jnp.where(labels == sibling_label, from_sibling[at].astype(F32), 0.0)
        part[at] = jnp.where(labels == amps_label, amps[at].astype(F32), other).astype(BF16).reshape(2, 2, 16, V)
    for chunk in range(2):
        for at, step in enumerate(STEPS):
            send(("ring", chunk), part.at[wrap(y, step, NY), :, chunk], from_ring.at[at, :, chunk], ("y", step))
    slab_start("sw", slab_w, (2,))

    def ring_end(chunk):
        arrive(("ring", chunk), from_ring.at[:, :, chunk])
        total = part[y, :, chunk]
        for at in range(len(STEPS)):
            total = total + from_ring[at, :, chunk]
        pair_a[pair, :, chunk] = total
        slab_a[slab, :, chunk] = total

    pair_turn("pw", pair_w, whole)
    for chunk in range(2):
        ring_end(chunk)
        pair_start("pa", pair_a, chunk)
    slab_start("sa", slab_a, STEPS)
    pair_turn("pa", pair_a, 0)
    slab_over("sw", slab_w)
    pair_turn("pa", pair_a, 1)
    slab_over("sa", slab_a)
    pair_own("pw", pair_w)
    pair_near("pw", pair_w)
    pair_far("pw", pair_w)
    slab_end("sw", slab_w)
    slab_end("sa", slab_a)

    def times(rows, every):
        return lax.dot_general(rows, every, (((1,), (1,)), ((), ())), preferred_element_type=F32)

    @pl.loop(0, 2)
    def _(at):
        half = NJ // 2
        rows = pair_w[pl.ds(at * half, half)].reshape(half * TILE, V)
        out_ref[0, pl.ds(at * half, half)] = times(rows, slab_a[...].reshape(V, V)).reshape(half, TILE, V)

    labels = pair_labels(slab) ^ own_label

    def second_term(group):
        rows = jnp.concatenate([pair_a[j].reshape(TILE, V) for j in group], axis=0)
        term = times(rows, slab_w[...].reshape(V, V))
        for at, j in enumerate(group):
            both = out_ref[0, j] + term[at * TILE : (at + 1) * TILE]
            out_ref[0, j] = jnp.where(labels == occ_ref[j], both, 0.0)

    pair_own("pa", pair_a)
    second_term([pair] + [beside(axis, step) for axis in ("x", "z") for step in STEPS])
    pair_near("pa", pair_a)
    second_term([beside("x", step, way) for step in NEAR for way in NEAR])
    pair_far("pa", pair_a)
    second_term([beside(axis, 2, way) for axis in ("x", "z") for way in NEAR] + [beside("x", 2, 2)])

    assert len(order) == N_SEMS
    assert sum(sent) == N_SENT
    copy("merge", spent, spent, "sibling").wait_send()


def solution(mesh):
    placed = (P("pair", "slab", None, None), P(None, "pair", "slab", None), P(), P(), P())
    piece = (2, 2, 16, V)

    def local(amplitudes, integrals, occ_irrep, slab_irrep, virt_irrep):
        operands = (
            amplitudes.reshape(NY, 2, TILE, V), integrals, occ_irrep.reshape(NJ), slab_irrep, virt_irrep.reshape(1, V)
        )
        return pl.pallas_call(
            kernel,
            out_shape=jax.ShapeDtypeStruct((1, NJ, TILE, V), F32),
            in_specs=[pl.BlockSpec(memory_space=pltpu.HBM)] * 5,
            out_specs=pl.BlockSpec(memory_space=pltpu.VMEM),
            scratch_shapes=[
                pltpu.VMEM((NY, TILE, V), BF16),
                pltpu.VMEM((8, TILE, V), BF16),
                pltpu.SMEM((NJ,), jnp.int32),
                pltpu.SMEM((8,), jnp.int32),
                pltpu.VMEM((1, V), jnp.int32),
                pltpu.VMEM((V, 128), jnp.int32),
                pltpu.VMEM((NY, TILE, V), BF16),
                pltpu.VMEM((NY, *piece), BF16),
                pltpu.VMEM((3, *piece), BF16),
                pltpu.VMEM((NJ, *piece), BF16),
                pltpu.VMEM((NJ, *piece), BF16),
                pltpu.VMEM((NS, *piece), BF16),
                pltpu.VMEM((NS, *piece), BF16),
                pltpu.VMEM((N_SENT, 16, V), BF16),
                pltpu.SemaphoreType.DMA((5,)),
                pltpu.SemaphoreType.DMA((1,)),
                pltpu.SemaphoreType.DMA((N_SEMS,)),
            ],
            compiler_params=pltpu.CompilerParams(
                collective_id=0, has_side_effects=True, vmem_limit_bytes=32 * 1024 * 1024
            ),
        )(*(pltpu.with_memory_space_constraint(operand, pltpu.HBM) for operand in operands))

    return jax.shard_map(
        local, mesh=mesh, in_specs=placed, out_specs=P("pair", None, "slab", None), check_vma=False
    )
```

```python
import jax
import jax.numpy as jnp
from jax import lax
from jax.experimental import pallas as pl
from jax.experimental.pallas import tpu as pltpu
from jax.sharding import PartitionSpec as P

NX = NY = NZ = 4
NJ = 16
NS = 8
TILE = 64
V = 512
N_SEMS = 25
N_SENT = 204
NEAR = (1, -1)
STEPS = (1, -1, 2)
BF16 = jnp.bfloat16
F32 = jnp.float32


def wrap(at, step, size):
    return lax.rem(at + step + size, size)


def kernel(
    amps_hbm, ints_hbm, occ_hbm, slab_hbm, virt_hbm, out_ref,
    amps, ints, occ_ref, slab_ref, virt_ref, row_labels, from_sibling, part, from_ring,
    pair_w, pair_a, slab_w, slab_a, spent, load_sems, send_sems, recv_sems,
):
    pair, slab = lax.axis_index("pair"), lax.axis_index("slab")
    z, x = pair // NX, lax.rem(pair, NX)
    y, core = slab // 2, lax.rem(slab, 2)
    sibling_core = 1 - core

    def at_pair(dz, dx):
        return wrap(z, dz, NZ) * NX + wrap(x, dx, NX)

    def at_slab(dy, own_core=True):
        return wrap(y, dy, NY) * 2 + (core if own_core else sibling_core)

    device = {"sibling": (pair, at_slab(0, False))}
    for step in (2, 1, -1):
        device["x", step] = (at_pair(0, step), slab)
        device["z", step] = (at_pair(step, 0), slab)
        device["y", step] = (pair, at_slab(step))

    loads = [
        pltpu.make_async_copy(src, dst, load_sems.at[at])
        for at, (src, dst) in enumerate((
            (virt_hbm, virt_ref),
            (occ_hbm, occ_ref),
            (slab_hbm, slab_ref),
            (amps_hbm.at[:, core], amps),
            (ints_hbm.at[:, 0], ints),
        ))
    ]

    barrier = pltpu.get_barrier_semaphore()
    for to in device.values():
        pl.semaphore_signal(barrier, inc=1, device_id=to, device_id_type=pl.DeviceIdType.MESH)

    for load in loads:
        load.start()

    order, sent = {}, []

    def copy(group, src, dst, to):
        at = order.setdefault(group, len(order))
        return pltpu.make_async_remote_copy(
            src_ref=src, dst_ref=dst, send_sem=send_sems.at[0], recv_sem=recv_sems.at[at],
            device_id=device[to], device_id_type=pl.DeviceIdType.MESH,
        )

    def send(group, src, dst, to):
        copy(group, src, dst, to).start()
        sent.append(src.size // (16 * V))

    def arrive(group, like):
        copy(group, like, like, "sibling").wait_recv()

    pl.semaphore_wait(barrier, len(device))
    send("merge", amps_hbm.at[:, sibling_core], from_sibling, "sibling")

    for load in loads[:3]:
        load.wait()
    columns = virt_ref[...]
    for at in range(V // 128):
        lanes = jnp.broadcast_to(columns[:, at * 128 : (at + 1) * 128], (128, 128))
        row_labels[at * 128 : (at + 1) * 128, :] = lanes.T

    def pair_labels(tile):
        rows = row_labels[pl.ds(pl.multiple_of(tile * TILE, TILE), TILE), :]
        return jnp.concatenate([rows] * (V // 128), axis=1) ^ columns

    own_label = occ_ref[pair]
    amps_label = own_label ^ slab_ref[slab]
    sibling_label = own_label ^ slab_ref[at_slab(0, False)]

    loads[4].wait()
    wanted = pair_labels(slab) ^ own_label
    w = jnp.zeros((TILE, V), F32)
    for k in range(8):
        w = jnp.where(wanted == slab_ref[k], ints[k].astype(F32), w)
    w = w.astype(BF16).reshape(2, 2, 16, V)
    pair_w[pair] = w
    slab_w[slab] = w

    axes = (("x", "z", 0), ("z", "x", 1))

    def beside(axis, step, other=0):
        return at_pair(other, step) if axis == "x" else at_pair(step, other)

    def start_far(tag, buf, chunk):
        for axis, _, _ in axes:
            own = buf.at[pair, :, chunk]
            send((tag, str(chunk), 2), own, own, (axis, 2))

    def start_near(tag, buf, chunk):
        for step in NEAR:
            for axis, _, half in axes:
                own = buf.at[pair, half, chunk]
                send((tag, str(chunk), 1), own, own, (axis, step))

    def start_own(tag, buf, chunk):
        for step in NEAR:
            for axis, _, half in axes:
                own = buf.at[pair, 1 - half, chunk]
                send((tag, "own"), own, own, (axis, step))

    def turn_near(tag, buf, chunk):
        arrive((tag, str(chunk), 1), buf.at[pl.ds(0, 2), :, chunk])
        for step in NEAR:
            for axis, other, half in axes:
                piece = buf.at[beside(axis, -step), half, chunk]
                for way in NEAR:
                    send((tag, "near"), piece, piece, (other, way))
    def turn_far(tag, buf, chunk):
        arrive((tag, str(chunk), 2), buf.at[pl.ds(0, 2), :, chunk])
        for axis, other, half in axes:
            piece = buf.at[beside(axis, 2), :, chunk]
            for way in NEAR:
                send((tag, "far"), piece, piece, (other, way))
            piece = buf.at[beside(axis, 2), half, chunk]
            send((tag, "far"), piece, piece, (other, 2))

    def pair_own(tag, buf):
        arrive((tag, "own"), buf.at[pl.ds(0, 2)])

    def pair_near(tag, buf):
        arrive((tag, "near"), buf.at[pl.ds(0, 4)])

    def pair_far(tag, buf):
        arrive((tag, "far"), buf.at[pl.ds(0, 5)])

    def slab_start(tag, buf, steps):
        for step in steps:
            send((tag, step), buf.at[slab], buf.at[slab], ("y", step))

    def slab_over(tag, buf):
        send((tag, "sibling"), buf.at[slab], buf.at[slab], "sibling")
        for step in STEPS:
            piece = buf.at[at_slab(-step)]
            arrive((tag, step), piece)
            send((tag, "sibling"), piece, piece, "sibling")

    def slab_end(tag, buf):
        arrive((tag, "sibling"), buf.at[pl.ds(0, NY)])

    whole = pl.ds(0, 2)
    start_far("pw", pair_w, 0)
    start_near("pw", pair_w, 0)
    start_far("pw", pair_w, 1)
    start_near("pw", pair_w, 1)
    start_own("pw", pair_w, whole)
    slab_start("sw", slab_w, NEAR)

    loads[3].wait()
    arrive("merge", from_sibling)
    for at in range(NY):
        labels = pair_labels(2 * at + core)
        other = jnp.where(labels == sibling_label, from_sibling[at].astype(F32), 0.0)
        part[at] = jnp.where(labels == amps_label, amps[at].astype(F32), other).astype(BF16).reshape(2, 2, 16, V)
    for chunk in range(2):
        for at, step in enumerate(STEPS):
            send(("ring", chunk), part.at[wrap(y, step, NY), :, chunk], from_ring.at[at, :, chunk], ("y", step))
    slab_start("sw", slab_w, (2,))

    def ring_end(chunk):
        arrive(("ring", chunk), from_ring.at[:, :, chunk])
        total = part[y, :, chunk]
        for at in range(len(STEPS)):
            total = total + from_ring[at, :, chunk]
        pair_a[pair, :, chunk] = total
        slab_a[slab, :, chunk] = total

    turn_near("pw", pair_w, 0)
    turn_far("pw", pair_w, 0)
    turn_near("pw", pair_w, 1)
    turn_far("pw", pair_w, 1)
    ring_end(0)
    start_far("pa", pair_a, 0)
    start_near("pa", pair_a, 0)
    ring_end(1)
    start_far("pa", pair_a, 1)
    start_near("pa", pair_a, 1)
    start_own("pa", pair_a, 0)
    start_own("pa", pair_a, 1)
    slab_start("sa", slab_a, STEPS)
    turn_far("pa", pair_a, 0)
    turn_near("pa", pair_a, 0)
    slab_over("sw", slab_w)
    turn_far("pa", pair_a, 1)
    turn_near("pa", pair_a, 1)

    slab_over("sa", slab_a)
    pair_own("pw", pair_w)
    pair_near("pw", pair_w)
    pair_far("pw", pair_w)
    slab_end("sw", slab_w)
    slab_end("sa", slab_a)

    def times(rows, every):
        return lax.dot_general(rows, every, (((1,), (1,)), ((), ())), preferred_element_type=F32)

    @pl.loop(0, 2)
    def _(at):
        half = NJ // 2
        rows = pair_w[pl.ds(at * half, half)].reshape(half * TILE, V)
        out_ref[0, pl.ds(at * half, half)] = times(rows, slab_a[...].reshape(V, V)).reshape(half, TILE, V)

    labels = pair_labels(slab) ^ own_label

    def second_term(group):
        rows = jnp.concatenate([pair_a[j].reshape(TILE, V) for j in group], axis=0)
        term = times(rows, slab_w[...].reshape(V, V))
        for at, j in enumerate(group):
            both = out_ref[0, j] + term[at * TILE : (at + 1) * TILE]
            out_ref[0, j] = jnp.where(labels == occ_ref[j], both, 0.0)

    pair_own("pa", pair_a)
    second_term([pair] + [beside(axis, step) for axis in ("x", "z") for step in STEPS])
    pair_near("pa", pair_a)
    second_term([beside("x", step, way) for step in NEAR for way in NEAR])
    pair_far("pa", pair_a)
    second_term([beside(axis, 2, way) for axis in ("x", "z") for way in NEAR] + [beside("x", 2, 2)])

    assert sum(sent) == N_SENT
    copy("merge", spent, spent, "sibling").wait_send()


def solution(mesh):
    placed = (P("pair", "slab", None, None), P(None, "pair", "slab", None), P(), P(), P())
    piece = (2, 2, 16, V)

    def local(amplitudes, integrals, occ_irrep, slab_irrep, virt_irrep):
        operands = (
            amplitudes.reshape(NY, 2, TILE, V), integrals, occ_irrep.reshape(NJ), slab_irrep, virt_irrep.reshape(1, V)
        )
        return pl.pallas_call(
            kernel,
            out_shape=jax.ShapeDtypeStruct((1, NJ, TILE, V), F32),
            in_specs=[pl.BlockSpec(memory_space=pltpu.HBM)] * 5,
            out_specs=pl.BlockSpec(memory_space=pltpu.VMEM),
            scratch_shapes=[
                pltpu.VMEM((NY, TILE, V), BF16),
                pltpu.VMEM((8, TILE, V), BF16),
                pltpu.SMEM((NJ,), jnp.int32),
                pltpu.SMEM((8,), jnp.int32),
                pltpu.VMEM((1, V), jnp.int32),
                pltpu.VMEM((V, 128), jnp.int32),
                pltpu.VMEM((NY, TILE, V), BF16),
                pltpu.VMEM((NY, *piece), BF16),
                pltpu.VMEM((3, *piece), BF16),
                pltpu.VMEM((NJ, *piece), BF16),
                pltpu.VMEM((NJ, *piece), BF16),
                pltpu.VMEM((NS, *piece), BF16),
                pltpu.VMEM((NS, *piece), BF16),
                pltpu.VMEM((N_SENT, 16, V), BF16),
                pltpu.SemaphoreType.DMA((5,)),
                pltpu.SemaphoreType.DMA((1,)),
                pltpu.SemaphoreType.DMA((N_SEMS,)),
            ],
            compiler_params=pltpu.CompilerParams(
                collective_id=0, has_side_effects=True, vmem_limit_bytes=32 * 1024 * 1024
            ),
        )(*(pltpu.with_memory_space_constraint(operand, pltpu.HBM) for operand in operands))

    return jax.shard_map(
        local, mesh=mesh, in_specs=placed, out_specs=P("pair", None, "slab", None), check_vma=False
    )
```

```python
import jax
import jax.numpy as jnp
from jax import lax
from jax.experimental import pallas as pl
from jax.experimental.pallas import tpu as pltpu
from jax.sharding import PartitionSpec as P

NX = NY = NZ = 4
NJ = 16
NS = 8
TILE = 64
V = 512
N_SEMS = 26
N_SENT = 204
NEAR = (1, -1)
STEPS = (1, -1, 2)
BF16 = jnp.bfloat16
F32 = jnp.float32


def wrap(at, step, size):
    return lax.rem(at + step + size, size)


def times(rows, every):
    return lax.dot_general(rows, every, (((1,), (1,)), ((), ())), preferred_element_type=F32)


def pieces_at(z, x, steps):
    return [wrap(z, dz, NZ) * NX + wrap(x, dx, NX) for dz, dx in steps]


def near_pieces(z, x):
    return pieces_at(z, x, [(0, 0)] + [(0, s) for s in STEPS] + [(s, 0) for s in STEPS] + [(a, b) for a in NEAR for b in NEAR])


def far_pieces(z, x):
    return pieces_at(z, x, [(2, s) for s in STEPS] + [(s, 2) for s in NEAR])


def finish(done_ref, rows_ref, every_ref, labels_ref, late_ref, out_hbm, last, sems):
    pair = lax.axis_index("pair")
    z, x = pair // NX, lax.rem(pair, NX)
    near, far = near_pieces(z, x), far_pieces(z, x)
    for j in near:
        pltpu.make_async_copy(done_ref.at[j], out_hbm.at[j], sems.at[0]).start()
    term = times(rows_ref[...], every_ref[...])
    for at, j in enumerate(far):
        kept = labels_ref[...] == jnp.concatenate([late_ref[at : at + 1, :]] * (V // 128), axis=1)
        last[at] = jnp.where(kept, done_ref[j] + term[at * TILE : (at + 1) * TILE], 0.0)
        pltpu.make_async_copy(last.at[at], out_hbm.at[j], sems.at[1]).start()
    many = done_ref.at[pl.ds(0, len(near))]
    pltpu.make_async_copy(many, out_hbm.at[pl.ds(0, len(near))], sems.at[0]).wait()
    pltpu.make_async_copy(last, out_hbm.at[pl.ds(0, len(far))], sems.at[1]).wait()


def kernel(
    amps_hbm, ints_hbm, occ_hbm, slab_hbm, virt_hbm, out_ref, rows_ref, every_ref, labels_ref, late_ref,
    amps, ints, occ_ref, slab_ref, virt_ref, row_labels, from_sibling, part, from_ring,
    pair_w, pair_a, slab_w, slab_a, spent, load_sems, send_sems, recv_sems,
):
    pair, slab = lax.axis_index("pair"), lax.axis_index("slab")
    z, x = pair // NX, lax.rem(pair, NX)
    y, core = slab // 2, lax.rem(slab, 2)
    sibling_core = 1 - core

    def at_pair(dz, dx):
        return wrap(z, dz, NZ) * NX + wrap(x, dx, NX)

    def at_slab(dy, own_core=True):
        return wrap(y, dy, NY) * 2 + (core if own_core else sibling_core)

    device = {"sibling": (pair, at_slab(0, False))}
    for step in (2, 1, -1):
        device["x", step] = (at_pair(0, step), slab)
        device["z", step] = (at_pair(step, 0), slab)
        device["y", step] = (pair, at_slab(step))

    loads = [
        pltpu.make_async_copy(src, dst, load_sems.at[at])
        for at, (src, dst) in enumerate((
            (virt_hbm, virt_ref),
            (occ_hbm, occ_ref),
            (slab_hbm, slab_ref),
            (amps_hbm.at[:, core], amps),
            (ints_hbm.at[:, 0], ints),
        ))
    ]

    barrier = pltpu.get_barrier_semaphore()
    for to in device.values():
        pl.semaphore_signal(barrier, inc=1, device_id=to, device_id_type=pl.DeviceIdType.MESH)

    for load in loads:
        load.start()

    order, sent = {}, []

    def copy(group, src, dst, to):
        at = order.setdefault(group, len(order))
        return pltpu.make_async_remote_copy(
            src_ref=src, dst_ref=dst, send_sem=send_sems.at[0], recv_sem=recv_sems.at[at],
            device_id=device[to], device_id_type=pl.DeviceIdType.MESH,
        )

    def send(group, src, dst, to):
        copy(group, src, dst, to).start()
        sent.append(src.size // (16 * V))

    def arrive(group, like):
        copy(group, like, like, "sibling").wait_recv()

    pl.semaphore_wait(barrier, len(device))
    for chunk in range(2):
        send(("merge", chunk), amps_hbm.at[:, sibling_core, :, chunk], from_sibling.at[:, :, chunk], "sibling")

    for load in loads[:3]:
        load.wait()
    columns = virt_ref[...]
    for at in range(V // 128):
        lanes = jnp.broadcast_to(columns[:, at * 128 : (at + 1) * 128], (128, 128))
        row_labels[at * 128 : (at + 1) * 128, :] = lanes.T

    def pair_labels(tile):
        rows = row_labels[pl.ds(pl.multiple_of(tile * TILE, TILE), TILE), :]
        return jnp.concatenate([rows] * (V // 128), axis=1) ^ columns

    own_label = occ_ref[pair]
    amps_label = own_label ^ slab_ref[slab]
    sibling_label = own_label ^ slab_ref[at_slab(0, False)]

    loads[4].wait()
    wanted = pair_labels(slab) ^ own_label
    w = jnp.zeros((TILE, V), F32)
    for k in range(8):
        w = jnp.where(wanted == slab_ref[k], ints[k].astype(F32), w)
    w = w.astype(BF16).reshape(2, 2, 16, V)
    pair_w[pair] = w
    slab_w[slab] = w

    axes = (("x", "z", 0), ("z", "x", 1))

    def beside(axis, step, other=0):
        return at_pair(other, step) if axis == "x" else at_pair(step, other)

    def start_far(tag, buf, chunk):
        for axis, _, _ in axes:
            own = buf.at[pair, :, chunk]
            send((tag, str(chunk), 2), own, own, (axis, 2))

    def start_near(tag, buf, chunk):
        for step in NEAR:
            for axis, _, half in axes:
                own = buf.at[pair, half, chunk]
                send((tag, str(chunk), 1), own, own, (axis, step))

    def start_own(tag, buf, chunk):
        for step in NEAR:
            for axis, _, half in axes:
                own = buf.at[pair, 1 - half, chunk]
                send((tag, "own"), own, own, (axis, step))

    def turn_near(tag, buf, chunk):
        arrive((tag, str(chunk), 1), buf.at[pl.ds(0, 2), :, chunk])
        for step in NEAR:
            for axis, other, half in axes:
                piece = buf.at[beside(axis, -step), half, chunk]
                for way in NEAR:
                    send((tag, "near"), piece, piece, (other, way))
    def turn_far(tag, buf, chunk):
        arrive((tag, str(chunk), 2), buf.at[pl.ds(0, 2), :, chunk])
        for axis, other, half in axes:
            piece = buf.at[beside(axis, 2), :, chunk]
            for way in NEAR:
                send((tag, "far"), piece, piece, (other, way))
            piece = buf.at[beside(axis, 2), half, chunk]
            send((tag, "far"), piece, piece, (other, 2))

    def pair_own(tag, buf):
        arrive((tag, "own"), buf.at[pl.ds(0, 2)])

    def pair_near(tag, buf):
        arrive((tag, "near"), buf.at[pl.ds(0, 4)])

    def pair_far(tag, buf):
        arrive((tag, "far"), buf.at[pl.ds(0, 5)])

    def slab_start(tag, buf, steps):
        for step in steps:
            send((tag, step), buf.at[slab], buf.at[slab], ("y", step))

    def slab_over(tag, buf):
        send((tag, "sibling"), buf.at[slab], buf.at[slab], "sibling")
        for step in STEPS:
            piece = buf.at[at_slab(-step)]
            arrive((tag, step), piece)
            send((tag, "sibling"), piece, piece, "sibling")

    def slab_end(tag, buf):
        arrive((tag, "sibling"), buf.at[pl.ds(0, NY)])

    whole = pl.ds(0, 2)
    start_far("pw", pair_w, 0)
    start_near("pw", pair_w, 0)
    start_far("pw", pair_w, 1)
    start_near("pw", pair_w, 1)
    start_own("pw", pair_w, whole)
    slab_start("sw", slab_w, NEAR)

    loads[3].wait()
    def merged(at, chunk):
        labels = pair_labels(2 * at + core).reshape(2, 2, 16, V)[:, chunk]
        other = jnp.where(labels == sibling_label, from_sibling[at, :, chunk].astype(F32), 0.0)
        return jnp.where(labels == amps_label, amps[at, :, chunk].astype(F32), other).astype(BF16)

    for chunk in range(2):
        arrive(("merge", chunk), from_sibling.at[:, :, chunk])
        for at, step in enumerate(STEPS):
            part[at, :, chunk] = merged(wrap(y, step, NY), chunk)
            send(("ring", chunk), part.at[at, :, chunk], from_ring.at[at, :, chunk], ("y", step))
    slab_start("sw", slab_w, (2,))

    def ring_end(chunk):
        total = merged(y, chunk)
        arrive(("ring", chunk), from_ring.at[:, :, chunk])
        for at in range(len(STEPS)):
            total = total + from_ring[at, :, chunk]
        pair_a[pair, :, chunk] = total
        slab_a[slab, :, chunk] = total

    turn_near("pw", pair_w, 0)
    turn_far("pw", pair_w, 0)
    turn_near("pw", pair_w, 1)
    turn_far("pw", pair_w, 1)
    ring_end(0)
    start_far("pa", pair_a, 0)
    start_near("pa", pair_a, 0)
    ring_end(1)
    start_far("pa", pair_a, 1)
    start_near("pa", pair_a, 1)
    start_own("pa", pair_a, 0)
    start_own("pa", pair_a, 1)
    slab_start("sa", slab_a, STEPS)
    turn_far("pa", pair_a, 0)
    turn_near("pa", pair_a, 0)
    slab_over("sw", slab_w)
    turn_far("pa", pair_a, 1)
    turn_near("pa", pair_a, 1)

    slab_over("sa", slab_a)
    pair_own("pw", pair_w)
    pair_near("pw", pair_w)
    pair_far("pw", pair_w)
    slab_end("sw", slab_w)
    slab_end("sa", slab_a)

    @pl.loop(0, 2)
    def _(at):
        half = NJ // 2
        rows = pair_w[pl.ds(at * half, half)].reshape(half * TILE, V)
        out_ref[pl.ds(at * half, half)] = times(rows, slab_a[...].reshape(V, V)).reshape(half, TILE, V)

    labels = pair_labels(slab) ^ own_label

    def second_term(group):
        rows = jnp.concatenate([pair_a[j].reshape(TILE, V) for j in group], axis=0)
        term = times(rows, slab_w[...].reshape(V, V))
        for at, j in enumerate(group):
            both = out_ref[j] + term[at * TILE : (at + 1) * TILE]
            out_ref[j] = jnp.where(labels == occ_ref[j], both, 0.0)

    pair_own("pa", pair_a)
    second_term([pair] + [beside(axis, step) for axis in ("x", "z") for step in STEPS])
    pair_near("pa", pair_a)
    second_term([beside("x", step, way) for step in NEAR for way in NEAR])
    every_ref[...] = slab_w[...].reshape(V, V)
    labels_ref[...] = labels
    for at, j in enumerate(far_pieces(z, x)):
        late_ref[at : at + 1, :] = jnp.full((1, 128), occ_ref[j], jnp.int32)
    pair_far("pa", pair_a)
    for at, j in enumerate(far_pieces(z, x)):
        rows_ref[at * TILE : (at + 1) * TILE, :] = pair_a[j].reshape(TILE, V)

    assert sum(sent) == N_SENT
    copy(("merge", 0), spent, spent, "sibling").wait_send()


def solution(mesh):
    placed = (P("pair", "slab", None, None), P(None, "pair", "slab", None), P(), P(), P())
    piece = (2, 2, 16, V)

    def local(amplitudes, integrals, occ_irrep, slab_irrep, virt_irrep):
        operands = (
            amplitudes.reshape(NY, 2, *piece), integrals, occ_irrep.reshape(NJ), slab_irrep, virt_irrep.reshape(1, V)
        )
        gathered = pl.pallas_call(
            kernel,
            out_shape=(
                jax.ShapeDtypeStruct((NJ, TILE, V), F32),
                jax.ShapeDtypeStruct((5 * TILE, V), BF16),
                jax.ShapeDtypeStruct((V, V), BF16),
                jax.ShapeDtypeStruct((TILE, V), jnp.int32),
                jax.ShapeDtypeStruct((8, 128), jnp.int32),
            ),
            in_specs=[pl.BlockSpec(memory_space=pltpu.HBM)] * 5,
            out_specs=[pl.BlockSpec(memory_space=pltpu.VMEM)] * 5,
            scratch_shapes=[
                pltpu.VMEM((NY, *piece), BF16),
                pltpu.VMEM((8, TILE, V), BF16),
                pltpu.SMEM((NJ,), jnp.int32),
                pltpu.SMEM((8,), jnp.int32),
                pltpu.VMEM((1, V), jnp.int32),
                pltpu.VMEM((V, 128), jnp.int32),
                pltpu.VMEM((NY, *piece), BF16),
                pltpu.VMEM((3, *piece), BF16),
                pltpu.VMEM((3, *piece), BF16),
                pltpu.VMEM((NJ, *piece), BF16),
                pltpu.VMEM((NJ, *piece), BF16),
                pltpu.VMEM((NS, *piece), BF16),
                pltpu.VMEM((NS, *piece), BF16),
                pltpu.VMEM((N_SENT, 16, V), BF16),
                pltpu.SemaphoreType.DMA((5,)),
                pltpu.SemaphoreType.DMA((1,)),
                pltpu.SemaphoreType.DMA((N_SEMS,)),
            ],
            compiler_params=pltpu.CompilerParams(
                collective_id=0, has_side_effects=True, vmem_limit_bytes=32 * 1024 * 1024
            ),
        )(*(pltpu.with_memory_space_constraint(operand, pltpu.HBM) for operand in operands))
        residual = pl.pallas_call(
            finish,
            out_shape=jax.ShapeDtypeStruct((NJ, TILE, V), F32),
            in_specs=[pl.BlockSpec(memory_space=pltpu.VMEM)] * 5,
            out_specs=pl.BlockSpec(memory_space=pltpu.HBM),
            scratch_shapes=[pltpu.VMEM((5, TILE, V), F32), pltpu.SemaphoreType.DMA((2,))],
            compiler_params=pltpu.CompilerParams(vmem_limit_bytes=16 * 1024 * 1024),
        )(*gathered)
        return residual[None]

    return jax.shard_map(
        local, mesh=mesh, in_specs=placed, out_specs=P("pair", None, "slab", None), check_vma=False
    )
```

```python
import jax
import jax.numpy as jnp
from jax import lax
from jax.experimental import pallas as pl
from jax.experimental.pallas import tpu as pltpu
from jax.sharding import PartitionSpec as P

NX = NY = NZ = 4
NJ = 16
NS = 8
TILE = 64
V = 512
N_SEMS = 26
N_SENT = 204
NEAR = (1, -1)
STEPS = (1, -1, 2)
BF16 = jnp.bfloat16
F32 = jnp.float32


def wrap(at, step, size):
    return lax.rem(at + step + size, size)


def times(rows, every):
    return lax.dot_general(rows, every, (((1,), (1,)), ((), ())), preferred_element_type=F32)


def pieces_at(z, x, steps):
    return [wrap(z, dz, NZ) * NX + wrap(x, dx, NX) for dz, dx in steps]


def near_pieces(z, x):
    return pieces_at(z, x, [(0, 0)] + [(0, s) for s in STEPS] + [(s, 0) for s in STEPS])


def far_pieces(z, x):
    return pieces_at(z, x, [(a, b) for a in NEAR for b in NEAR] + [(2, s) for s in STEPS] + [(s, 2) for s in NEAR])


def finish(done_ref, rows_ref, every_ref, labels_ref, late_ref, out_hbm, last, sems):
    pair = lax.axis_index("pair")
    z, x = pair // NX, lax.rem(pair, NX)
    near, far = near_pieces(z, x), far_pieces(z, x)
    for j in near:
        pltpu.make_async_copy(done_ref.at[j], out_hbm.at[j], sems.at[0]).start()
    for first, after in ((0, 4), (4, 9)):
        term = times(rows_ref[first * TILE : after * TILE, :], every_ref[...])
        for at in range(first, after):
            kept = labels_ref[...] == jnp.concatenate([late_ref[at : at + 1, :]] * (V // 128), axis=1)
            both = done_ref[far[at]] + term[(at - first) * TILE : (at - first + 1) * TILE]
            last[at] = jnp.where(kept, both, 0.0)
            pltpu.make_async_copy(last.at[at], out_hbm.at[far[at]], sems.at[1]).start()
    many = done_ref.at[pl.ds(0, len(near))]
    pltpu.make_async_copy(many, out_hbm.at[pl.ds(0, len(near))], sems.at[0]).wait()
    pltpu.make_async_copy(last, out_hbm.at[pl.ds(0, len(far))], sems.at[1]).wait()


def kernel(
    amps_hbm, ints_hbm, occ_hbm, slab_hbm, virt_hbm, out_ref, rows_ref, every_ref, labels_ref, late_ref,
    amps, ints, occ_ref, slab_ref, virt_ref, row_labels, from_sibling, part, from_ring,
    pair_w, pair_a, slab_w, slab_a, spent, load_sems, send_sems, recv_sems,
):
    pair, slab = lax.axis_index("pair"), lax.axis_index("slab")
    z, x = pair // NX, lax.rem(pair, NX)
    y, core = slab // 2, lax.rem(slab, 2)
    sibling_core = 1 - core

    def at_pair(dz, dx):
        return wrap(z, dz, NZ) * NX + wrap(x, dx, NX)

    def at_slab(dy, own_core=True):
        return wrap(y, dy, NY) * 2 + (core if own_core else sibling_core)

    device = {"sibling": (pair, at_slab(0, False))}
    for step in (2, 1, -1):
        device["x", step] = (at_pair(0, step), slab)
        device["z", step] = (at_pair(step, 0), slab)
        device["y", step] = (pair, at_slab(step))

    loads = [
        pltpu.make_async_copy(src, dst, load_sems.at[at])
        for at, (src, dst) in enumerate((
            (virt_hbm, virt_ref),
            (occ_hbm, occ_ref),
            (slab_hbm, slab_ref),
            (amps_hbm.at[:, core], amps),
            (ints_hbm.at[:, 0], ints),
        ))
    ]

    barrier = pltpu.get_barrier_semaphore()
    for to in device.values():
        pl.semaphore_signal(barrier, inc=1, device_id=to, device_id_type=pl.DeviceIdType.MESH)

    for load in loads:
        load.start()

    order, sent = {}, []

    def copy(group, src, dst, to):
        at = order.setdefault(group, len(order))
        return pltpu.make_async_remote_copy(
            src_ref=src, dst_ref=dst, send_sem=send_sems.at[0], recv_sem=recv_sems.at[at],
            device_id=device[to], device_id_type=pl.DeviceIdType.MESH,
        )

    def send(group, src, dst, to):
        copy(group, src, dst, to).start()
        sent.append(src.size // (16 * V))

    def arrive(group, like):
        copy(group, like, like, "sibling").wait_recv()

    pl.semaphore_wait(barrier, len(device))
    for chunk in range(2):
        send(("merge", chunk), amps_hbm.at[:, sibling_core, :, chunk], from_sibling.at[:, :, chunk], "sibling")

    for load in loads[:3]:
        load.wait()
    columns = virt_ref[...]
    for at in range(V // 128):
        lanes = jnp.broadcast_to(columns[:, at * 128 : (at + 1) * 128], (128, 128))
        row_labels[at * 128 : (at + 1) * 128, :] = lanes.T

    def pair_labels(tile):
        rows = row_labels[pl.ds(pl.multiple_of(tile * TILE, TILE), TILE), :]
        return jnp.concatenate([rows] * (V // 128), axis=1) ^ columns

    own_label = occ_ref[pair]
    amps_label = own_label ^ slab_ref[slab]
    sibling_label = own_label ^ slab_ref[at_slab(0, False)]

    loads[4].wait()
    wanted = pair_labels(slab) ^ own_label
    w = jnp.zeros((TILE, V), F32)
    for k in range(8):
        w = jnp.where(wanted == slab_ref[k], ints[k].astype(F32), w)
    w = w.astype(BF16).reshape(2, 2, 16, V)
    pair_w[pair] = w
    slab_w[slab] = w

    axes = (("x", "z", 0), ("z", "x", 1))

    def beside(axis, step, other=0):
        return at_pair(other, step) if axis == "x" else at_pair(step, other)

    def start_far(tag, buf, chunk):
        for axis, _, _ in axes:
            own = buf.at[pair, :, chunk]
            send((tag, str(chunk), 2), own, own, (axis, 2))

    def start_near(tag, buf, chunk):
        for step in NEAR:
            for axis, _, half in axes:
                own = buf.at[pair, half, chunk]
                send((tag, str(chunk), 1), own, own, (axis, step))

    def start_own(tag, buf, chunk):
        for step in NEAR:
            for axis, _, half in axes:
                own = buf.at[pair, 1 - half, chunk]
                send((tag, "own"), own, own, (axis, step))

    def turn_near(tag, buf, chunk):
        arrive((tag, str(chunk), 1), buf.at[pl.ds(0, 2), :, chunk])
        for step in NEAR:
            for axis, other, half in axes:
                piece = buf.at[beside(axis, -step), half, chunk]
                for way in NEAR:
                    send((tag, "near"), piece, piece, (other, way))
    def turn_far(tag, buf, chunk):
        arrive((tag, str(chunk), 2), buf.at[pl.ds(0, 2), :, chunk])
        for axis, other, half in axes:
            piece = buf.at[beside(axis, 2), :, chunk]
            for way in NEAR:
                send((tag, "far"), piece, piece, (other, way))
            piece = buf.at[beside(axis, 2), half, chunk]
            send((tag, "far"), piece, piece, (other, 2))

    def pair_own(tag, buf):
        arrive((tag, "own"), buf.at[pl.ds(0, 2)])

    def pair_near(tag, buf):
        arrive((tag, "near"), buf.at[pl.ds(0, 4)])

    def pair_far(tag, buf):
        arrive((tag, "far"), buf.at[pl.ds(0, 5)])

    def slab_start(tag, buf, steps):
        for step in steps:
            send((tag, step), buf.at[slab], buf.at[slab], ("y", step))

    def slab_over(tag, buf):
        send((tag, "sibling"), buf.at[slab], buf.at[slab], "sibling")
        for step in STEPS:
            piece = buf.at[at_slab(-step)]
            arrive((tag, step), piece)
            send((tag, "sibling"), piece, piece, "sibling")

    def slab_end(tag, buf):
        arrive((tag, "sibling"), buf.at[pl.ds(0, NY)])

    whole = pl.ds(0, 2)
    start_far("pw", pair_w, 0)
    start_near("pw", pair_w, 0)
    start_far("pw", pair_w, 1)
    start_near("pw", pair_w, 1)
    start_own("pw", pair_w, whole)
    slab_start("sw", slab_w, NEAR)

    loads[3].wait()
    def merged(at, chunk):
        labels = pair_labels(2 * at + core).reshape(2, 2, 16, V)[:, chunk]
        other = jnp.where(labels == sibling_label, from_sibling[at, :, chunk].astype(F32), 0.0)
        return jnp.where(labels == amps_label, amps[at, :, chunk].astype(F32), other).astype(BF16)

    for chunk in range(2):
        arrive(("merge", chunk), from_sibling.at[:, :, chunk])
        for at, step in enumerate(STEPS):
            part[at, :, chunk] = merged(wrap(y, step, NY), chunk)
            send(("ring", chunk), part.at[at, :, chunk], from_ring.at[at, :, chunk], ("y", step))
    slab_start("sw", slab_w, (2,))

    def ring_end(chunk):
        total = merged(y, chunk)
        arrive(("ring", chunk), from_ring.at[:, :, chunk])
        for at in range(len(STEPS)):
            total = total + from_ring[at, :, chunk]
        pair_a[pair, :, chunk] = total
        slab_a[slab, :, chunk] = total

    turn_near("pw", pair_w, 0)
    turn_far("pw", pair_w, 0)
    turn_near("pw", pair_w, 1)
    turn_far("pw", pair_w, 1)
    ring_end(0)
    start_far("pa", pair_a, 0)
    start_near("pa", pair_a, 0)
    ring_end(1)
    start_far("pa", pair_a, 1)
    start_near("pa", pair_a, 1)
    start_own("pa", pair_a, 0)
    start_own("pa", pair_a, 1)
    slab_start("sa", slab_a, STEPS)
    turn_far("pa", pair_a, 0)
    turn_near("pa", pair_a, 0)
    slab_over("sw", slab_w)
    turn_far("pa", pair_a, 1)
    turn_near("pa", pair_a, 1)

    slab_over("sa", slab_a)
    pair_own("pw", pair_w)
    pair_near("pw", pair_w)
    pair_far("pw", pair_w)
    slab_end("sw", slab_w)
    slab_end("sa", slab_a)

    @pl.loop(0, 2)
    def _(at):
        half = NJ // 2
        rows = pair_w[pl.ds(at * half, half)].reshape(half * TILE, V)
        out_ref[pl.ds(at * half, half)] = times(rows, slab_a[...].reshape(V, V)).reshape(half, TILE, V)

    labels = pair_labels(slab) ^ own_label

    def second_term(group):
        rows = jnp.concatenate([pair_a[j].reshape(TILE, V) for j in group], axis=0)
        term = times(rows, slab_w[...].reshape(V, V))
        for at, j in enumerate(group):
            both = out_ref[j] + term[at * TILE : (at + 1) * TILE]
            out_ref[j] = jnp.where(labels == occ_ref[j], both, 0.0)

    pair_own("pa", pair_a)
    second_term([pair] + [beside(axis, step) for axis in ("x", "z") for step in STEPS])
    every_ref[...] = slab_w[...].reshape(V, V)
    labels_ref[...] = labels
    for at, j in enumerate(far_pieces(z, x)):
        late_ref[at : at + 1, :] = jnp.full((1, 128), occ_ref[j], jnp.int32)
    pair_near("pa", pair_a)
    for at, j in enumerate(far_pieces(z, x)):
        if at == 4:
            pair_far("pa", pair_a)
        rows_ref[at * TILE : (at + 1) * TILE, :] = pair_a[j].reshape(TILE, V)

    assert sum(sent) == N_SENT
    copy(("merge", 0), spent, spent, "sibling").wait_send()


def solution(mesh):
    placed = (P("pair", "slab", None, None), P(None, "pair", "slab", None), P(), P(), P())
    piece = (2, 2, 16, V)

    def local(amplitudes, integrals, occ_irrep, slab_irrep, virt_irrep):
        operands = (
            amplitudes.reshape(NY, 2, *piece), integrals, occ_irrep.reshape(NJ), slab_irrep, virt_irrep.reshape(1, V)
        )
        gathered = pl.pallas_call(
            kernel,
            out_shape=(
                jax.ShapeDtypeStruct((NJ, TILE, V), F32),
                jax.ShapeDtypeStruct((9 * TILE, V), BF16),
                jax.ShapeDtypeStruct((V, V), BF16),
                jax.ShapeDtypeStruct((TILE, V), jnp.int32),
                jax.ShapeDtypeStruct((16, 128), jnp.int32),
            ),
            in_specs=[pl.BlockSpec(memory_space=pltpu.HBM)] * 5,
            out_specs=[pl.BlockSpec(memory_space=pltpu.VMEM)] * 5,
            scratch_shapes=[
                pltpu.VMEM((NY, *piece), BF16),
                pltpu.VMEM((8, TILE, V), BF16),
                pltpu.SMEM((NJ,), jnp.int32),
                pltpu.SMEM((8,), jnp.int32),
                pltpu.VMEM((1, V), jnp.int32),
                pltpu.VMEM((V, 128), jnp.int32),
                pltpu.VMEM((NY, *piece), BF16),
                pltpu.VMEM((3, *piece), BF16),
                pltpu.VMEM((3, *piece), BF16),
                pltpu.VMEM((NJ, *piece), BF16),
                pltpu.VMEM((NJ, *piece), BF16),
                pltpu.VMEM((NS, *piece), BF16),
                pltpu.VMEM((NS, *piece), BF16),
                pltpu.VMEM((N_SENT, 16, V), BF16),
                pltpu.SemaphoreType.DMA((5,)),
                pltpu.SemaphoreType.DMA((1,)),
                pltpu.SemaphoreType.DMA((N_SEMS,)),
            ],
            compiler_params=pltpu.CompilerParams(
                collective_id=0, has_side_effects=True, vmem_limit_bytes=32 * 1024 * 1024
            ),
        )(*(pltpu.with_memory_space_constraint(operand, pltpu.HBM) for operand in operands))
        residual = pl.pallas_call(
            finish,
            out_shape=jax.ShapeDtypeStruct((NJ, TILE, V), F32),
            in_specs=[pl.BlockSpec(memory_space=pltpu.VMEM)] * 5,
            out_specs=pl.BlockSpec(memory_space=pltpu.HBM),
            scratch_shapes=[pltpu.VMEM((9, TILE, V), F32), pltpu.SemaphoreType.DMA((2,))],
            compiler_params=pltpu.CompilerParams(vmem_limit_bytes=16 * 1024 * 1024),
        )(*gathered)
        return residual[None]

    return jax.shard_map(
        local, mesh=mesh, in_specs=placed, out_specs=P("pair", None, "slab", None), check_vma=False
    )
```

```python
import jax
import jax.numpy as jnp
from jax import lax
from jax.experimental import pallas as pl
from jax.experimental.pallas import tpu as pltpu
from jax.sharding import PartitionSpec as P

NX = NY = NZ = 4
NJ = 16
NS = 8
TILE = 64
V = 512
N_SEMS = 26
N_SENT = 204
NEAR = (1, -1)
STEPS = (1, -1, 2)
BF16 = jnp.bfloat16
F32 = jnp.float32


def wrap(at, step, size):
    return lax.rem(at + step + size, size)


def times(rows, every):
    return lax.dot_general(rows, every, (((1,), (1,)), ((), ())), preferred_element_type=F32)


def pieces_at(z, x, steps):
    return [wrap(z, dz, NZ) * NX + wrap(x, dx, NX) for dz, dx in steps]


def near_pieces(z, x):
    return pieces_at(z, x, [(0, 0)] + [(0, s) for s in STEPS] + [(s, 0) for s in STEPS])


def far_pieces(z, x):
    return pieces_at(z, x, [(a, b) for a in NEAR for b in NEAR] + [(2, s) for s in STEPS] + [(s, 2) for s in NEAR])


def finish(done_ref, rows_ref, every_ref, labels_ref, late_ref, out_hbm, last, sems):
    pair = lax.axis_index("pair")
    z, x = pair // NX, lax.rem(pair, NX)
    near, far = near_pieces(z, x), far_pieces(z, x)
    for j in near:
        pltpu.make_async_copy(done_ref.at[j], out_hbm.at[j], sems.at[0]).start()
    for first, after in ((0, 4), (4, 9)):
        term = times(rows_ref[first * TILE : after * TILE, :], every_ref[...])
        for at in range(first, after):
            kept = labels_ref[...] == jnp.concatenate([late_ref[at : at + 1, :]] * (V // 128), axis=1)
            both = done_ref[far[at]] + term[(at - first) * TILE : (at - first + 1) * TILE]
            last[at] = jnp.where(kept, both, 0.0)
            pltpu.make_async_copy(last.at[at], out_hbm.at[far[at]], sems.at[1]).start()
    many = done_ref.at[pl.ds(0, len(near))]
    pltpu.make_async_copy(many, out_hbm.at[pl.ds(0, len(near))], sems.at[0]).wait()
    pltpu.make_async_copy(last, out_hbm.at[pl.ds(0, len(far))], sems.at[1]).wait()


def kernel(
    amps_hbm, ints_hbm, occ_hbm, slab_hbm, virt_hbm, out_ref, rows_ref, every_ref, labels_ref, late_ref,
    amps, ints, occ_ref, slab_ref, virt_ref, row_labels, from_sibling, part, from_ring,
    pair_w, pair_a, slab_w, slab_a, spent, load_sems, send_sems, recv_sems,
):
    pair, slab = lax.axis_index("pair"), lax.axis_index("slab")
    z, x = pair // NX, lax.rem(pair, NX)
    y, core = slab // 2, lax.rem(slab, 2)
    sibling_core = 1 - core

    def at_pair(dz, dx):
        return wrap(z, dz, NZ) * NX + wrap(x, dx, NX)

    def at_slab(dy, own_core=True):
        return wrap(y, dy, NY) * 2 + (core if own_core else sibling_core)

    device = {"sibling": (pair, at_slab(0, False))}
    for step in (2, 1, -1):
        device["x", step] = (at_pair(0, step), slab)
        device["z", step] = (at_pair(step, 0), slab)
        device["y", step] = (pair, at_slab(step))

    loads = [
        pltpu.make_async_copy(src, dst, load_sems.at[at])
        for at, (src, dst) in enumerate((
            (virt_hbm, virt_ref),
            (occ_hbm, occ_ref),
            (slab_hbm, slab_ref),
            (amps_hbm.at[:, core], amps),
            (ints_hbm.at[:, 0], ints),
        ))
    ]

    barrier = pltpu.get_barrier_semaphore()
    for to in device.values():
        pl.semaphore_signal(barrier, inc=1, device_id=to, device_id_type=pl.DeviceIdType.MESH)

    for load in loads:
        load.start()

    order, sent = {}, []

    def copy(group, src, dst, to):
        at = order.setdefault(group, len(order))
        return pltpu.make_async_remote_copy(
            src_ref=src, dst_ref=dst, send_sem=send_sems.at[0], recv_sem=recv_sems.at[at],
            device_id=device[to], device_id_type=pl.DeviceIdType.MESH,
        )

    def send(group, src, dst, to):
        copy(group, src, dst, to).start()
        sent.append(src.size // (16 * V))

    def arrive(group, like):
        copy(group, like, like, "sibling").wait_recv()

    pl.semaphore_wait(barrier, len(device))
    for chunk in range(2):
        send(("merge", chunk), amps_hbm.at[:, sibling_core, :, chunk], from_sibling.at[:, :, chunk], "sibling")

    for load in loads[:3]:
        load.wait()
    columns = virt_ref[...]
    for at in range(V // 128):
        lanes = jnp.broadcast_to(columns[:, at * 128 : (at + 1) * 128], (128, 128))
        row_labels[at * 128 : (at + 1) * 128, :] = lanes.T

    def pair_labels(tile):
        rows = row_labels[pl.ds(pl.multiple_of(tile * TILE, TILE), TILE), :]
        return jnp.concatenate([rows] * (V // 128), axis=1) ^ columns

    own_label = occ_ref[pair]
    amps_label = own_label ^ slab_ref[slab]
    sibling_label = own_label ^ slab_ref[at_slab(0, False)]

    loads[4].wait()
    wanted = pair_labels(slab) ^ own_label
    w = jnp.zeros((TILE, V), F32)
    for k in range(8):
        w = jnp.where(wanted == slab_ref[k], ints[k].astype(F32), w)
    w = w.astype(BF16).reshape(2, 2, 16, V)
    pair_w[pair] = w
    slab_w[slab] = w

    axes = (("x", "z", 0), ("z", "x", 1))

    def beside(axis, step, other=0):
        return at_pair(other, step) if axis == "x" else at_pair(step, other)

    def start_far(tag, buf, chunk):
        for axis, _, _ in axes:
            own = buf.at[pair, :, chunk]
            send((tag, str(chunk), 2), own, own, (axis, 2))

    def start_near(tag, buf, chunk):
        for step in NEAR:
            for axis, _, half in axes:
                own = buf.at[pair, half, chunk]
                send((tag, str(chunk), 1), own, own, (axis, step))

    def start_own(tag, buf, chunk):
        for step in NEAR:
            for axis, _, half in axes:
                own = buf.at[pair, 1 - half, chunk]
                send((tag, "own"), own, own, (axis, step))

    def turn_near(tag, buf, chunk):
        arrive((tag, str(chunk), 1), buf.at[pl.ds(0, 2), :, chunk])
        for step in NEAR:
            for axis, other, half in axes:
                piece = buf.at[beside(axis, -step), half, chunk]
                for way in NEAR:
                    send((tag, "near"), piece, piece, (other, way))
    def turn_far(tag, buf, chunk):
        arrive((tag, str(chunk), 2), buf.at[pl.ds(0, 2), :, chunk])
        for axis, other, half in axes:
            piece = buf.at[beside(axis, 2), :, chunk]
            for way in NEAR:
                send((tag, "far"), piece, piece, (other, way))
            piece = buf.at[beside(axis, 2), half, chunk]
            send((tag, "far"), piece, piece, (other, 2))

    def pair_own(tag, buf):
        arrive((tag, "own"), buf.at[pl.ds(0, 2)])

    def pair_near(tag, buf):
        arrive((tag, "near"), buf.at[pl.ds(0, 4)])

    def pair_far(tag, buf):
        arrive((tag, "far"), buf.at[pl.ds(0, 5)])

    def slab_start(tag, buf, steps):
        for step in steps:
            send((tag, step), buf.at[slab], buf.at[slab], ("y", step))

    def slab_over(tag, buf):
        send((tag, "sibling"), buf.at[slab], buf.at[slab], "sibling")
        for step in STEPS:
            piece = buf.at[at_slab(-step)]
            arrive((tag, step), piece)
            send((tag, "sibling"), piece, piece, "sibling")

    def slab_end(tag, buf):
        arrive((tag, "sibling"), buf.at[pl.ds(0, NY)])

    whole = pl.ds(0, 2)
    start_far("pw", pair_w, 0)
    start_near("pw", pair_w, 0)
    start_far("pw", pair_w, 1)
    start_near("pw", pair_w, 1)
    slab_start("sw", slab_w, NEAR)

    loads[3].wait()
    def merged(at, chunk):
        labels = pair_labels(2 * at + core).reshape(2, 2, 16, V)[:, chunk]
        other = jnp.where(labels == sibling_label, from_sibling[at, :, chunk].astype(F32), 0.0)
        return jnp.where(labels == amps_label, amps[at, :, chunk].astype(F32), other).astype(BF16)

    for chunk in range(2):
        arrive(("merge", chunk), from_sibling.at[:, :, chunk])
        for at, step in enumerate(STEPS):
            part[at, :, chunk] = merged(wrap(y, step, NY), chunk)
            send(("ring", chunk), part.at[at, :, chunk], from_ring.at[at, :, chunk], ("y", step))
    slab_start("sw", slab_w, (2,))
    start_own("pw", pair_w, whole)

    def ring_end(chunk):
        total = merged(y, chunk)
        arrive(("ring", chunk), from_ring.at[:, :, chunk])
        for at in range(len(STEPS)):
            total = total + from_ring[at, :, chunk]
        pair_a[pair, :, chunk] = total
        slab_a[slab, :, chunk] = total

    turn_near("pw", pair_w, 0)
    turn_far("pw", pair_w, 0)
    turn_near("pw", pair_w, 1)
    turn_far("pw", pair_w, 1)
    ring_end(0)
    start_far("pa", pair_a, 0)
    start_near("pa", pair_a, 0)
    ring_end(1)
    start_far("pa", pair_a, 1)
    start_near("pa", pair_a, 1)
    start_own("pa", pair_a, 0)
    start_own("pa", pair_a, 1)
    slab_start("sa", slab_a, STEPS)
    turn_far("pa", pair_a, 0)
    turn_near("pa", pair_a, 0)
    slab_over("sw", slab_w)
    turn_far("pa", pair_a, 1)
    turn_near("pa", pair_a, 1)

    slab_over("sa", slab_a)
    pair_own("pw", pair_w)
    pair_near("pw", pair_w)
    pair_far("pw", pair_w)
    slab_end("sw", slab_w)
    slab_end("sa", slab_a)

    @pl.loop(0, 2)
    def _(at):
        half = NJ // 2
        rows = pair_w[pl.ds(at * half, half)].reshape(half * TILE, V)
        out_ref[pl.ds(at * half, half)] = times(rows, slab_a[...].reshape(V, V)).reshape(half, TILE, V)

    labels = pair_labels(slab) ^ own_label

    def second_term(group):
        rows = jnp.concatenate([pair_a[j].reshape(TILE, V) for j in group], axis=0)
        term = times(rows, slab_w[...].reshape(V, V))
        for at, j in enumerate(group):
            both = out_ref[j] + term[at * TILE : (at + 1) * TILE]
            out_ref[j] = jnp.where(labels == occ_ref[j], both, 0.0)

    pair_own("pa", pair_a)
    second_term([pair] + [beside(axis, step) for axis in ("x", "z") for step in STEPS])
    every_ref[...] = slab_w[...].reshape(V, V)
    labels_ref[...] = labels
    for at, j in enumerate(far_pieces(z, x)):
        late_ref[at : at + 1, :] = jnp.full((1, 128), occ_ref[j], jnp.int32)
    pair_near("pa", pair_a)
    for at, j in enumerate(far_pieces(z, x)):
        if at == 4:
            pair_far("pa", pair_a)
        rows_ref[at * TILE : (at + 1) * TILE, :] = pair_a[j].reshape(TILE, V)

    assert sum(sent) == N_SENT
    copy(("merge", 0), spent, spent, "sibling").wait_send()


def solution(mesh):
    placed = (P("pair", "slab", None, None), P(None, "pair", "slab", None), P(), P(), P())
    piece = (2, 2, 16, V)

    def local(amplitudes, integrals, occ_irrep, slab_irrep, virt_irrep):
        operands = (
            amplitudes.reshape(NY, 2, *piece), integrals, occ_irrep.reshape(NJ), slab_irrep, virt_irrep.reshape(1, V)
        )
        gathered = pl.pallas_call(
            kernel,
            out_shape=(
                jax.ShapeDtypeStruct((NJ, TILE, V), F32),
                jax.ShapeDtypeStruct((9 * TILE, V), BF16),
                jax.ShapeDtypeStruct((V, V), BF16),
                jax.ShapeDtypeStruct((TILE, V), jnp.int32),
                jax.ShapeDtypeStruct((16, 128), jnp.int32),
            ),
            in_specs=[pl.BlockSpec(memory_space=pltpu.HBM)] * 5,
            out_specs=[pl.BlockSpec(memory_space=pltpu.VMEM)] * 5,
            scratch_shapes=[
                pltpu.VMEM((NY, *piece), BF16),
                pltpu.VMEM((8, TILE, V), BF16),
                pltpu.SMEM((NJ,), jnp.int32),
                pltpu.SMEM((8,), jnp.int32),
                pltpu.VMEM((1, V), jnp.int32),
                pltpu.VMEM((V, 128), jnp.int32),
                pltpu.VMEM((NY, *piece), BF16),
                pltpu.VMEM((3, *piece), BF16),
                pltpu.VMEM((3, *piece), BF16),
                pltpu.VMEM((NJ, *piece), BF16),
                pltpu.VMEM((NJ, *piece), BF16),
                pltpu.VMEM((NS, *piece), BF16),
                pltpu.VMEM((NS, *piece), BF16),
                pltpu.VMEM((N_SENT, 16, V), BF16),
                pltpu.SemaphoreType.DMA((5,)),
                pltpu.SemaphoreType.DMA((1,)),
                pltpu.SemaphoreType.DMA((N_SEMS,)),
            ],
            compiler_params=pltpu.CompilerParams(
                collective_id=0, has_side_effects=True, vmem_limit_bytes=32 * 1024 * 1024
            ),
        )(*(pltpu.with_memory_space_constraint(operand, pltpu.HBM) for operand in operands))
        residual = pl.pallas_call(
            finish,
            out_shape=jax.ShapeDtypeStruct((NJ, TILE, V), F32),
            in_specs=[pl.BlockSpec(memory_space=pltpu.VMEM)] * 5,
            out_specs=pl.BlockSpec(memory_space=pltpu.HBM),
            scratch_shapes=[pltpu.VMEM((9, TILE, V), F32), pltpu.SemaphoreType.DMA((2,))],
            compiler_params=pltpu.CompilerParams(vmem_limit_bytes=16 * 1024 * 1024),
        )(*gathered)
        return residual[None]

    return jax.shard_map(
        local, mesh=mesh, in_specs=placed, out_specs=P("pair", None, "slab", None), check_vma=False
    )
```

```python
import jax
import jax.numpy as jnp
from jax import lax
from jax.experimental import pallas as pl
from jax.experimental.pallas import tpu as pltpu
from jax.sharding import PartitionSpec as P

NX = NY = NZ = 4
NJ = 16
NS = 8
TILE = 64
V = 512
N_SEMS = 26
N_SENT = 204
NEAR = (1, -1)
STEPS = (1, -1, 2)
BF16 = jnp.bfloat16
F32 = jnp.float32


def wrap(at, step, size):
    return lax.rem(at + step + size, size)


def times(rows, every):
    return lax.dot_general(rows, every, (((1,), (1,)), ((), ())), preferred_element_type=F32)


def pieces_at(z, x, steps):
    return [wrap(z, dz, NZ) * NX + wrap(x, dx, NX) for dz, dx in steps]


def near_pieces(z, x):
    return pieces_at(z, x, [(0, 0)] + [(0, s) for s in STEPS] + [(s, 0) for s in STEPS])


def far_pieces(z, x):
    return pieces_at(z, x, [(a, b) for a in NEAR for b in NEAR] + [(2, s) for s in STEPS] + [(s, 2) for s in NEAR])


def finish(done_ref, rows_ref, every_ref, labels_ref, late_ref, out_hbm, last, sems):
    pair = lax.axis_index("pair")
    z, x = pair // NX, lax.rem(pair, NX)
    near, far = near_pieces(z, x), far_pieces(z, x)
    for j in near:
        pltpu.make_async_copy(done_ref.at[j], out_hbm.at[j], sems.at[0]).start()
    for first, after in ((0, 4), (4, 9)):
        term = times(rows_ref[first * TILE : after * TILE, :], every_ref[...])
        for at in range(first, after):
            kept = labels_ref[...] == jnp.concatenate([late_ref[at : at + 1, :]] * (V // 128), axis=1)
            both = done_ref[far[at]] + term[(at - first) * TILE : (at - first + 1) * TILE]
            last[at] = jnp.where(kept, both, 0.0)
            pltpu.make_async_copy(last.at[at], out_hbm.at[far[at]], sems.at[1]).start()
    many = done_ref.at[pl.ds(0, len(near))]
    pltpu.make_async_copy(many, out_hbm.at[pl.ds(0, len(near))], sems.at[0]).wait()
    pltpu.make_async_copy(last, out_hbm.at[pl.ds(0, len(far))], sems.at[1]).wait()


def kernel(
    amps_hbm, ints_hbm, occ_hbm, slab_hbm, virt_hbm, out_ref, rows_ref, every_ref, labels_ref, late_ref,
    amps, ints, occ_ref, slab_ref, virt_ref, row_labels, to_sibling, from_sibling, part, from_ring,
    pair_w, pair_a, slab_w, slab_a, spent, load_sems, send_sems, recv_sems,
):
    pair, slab = lax.axis_index("pair"), lax.axis_index("slab")
    z, x = pair // NX, lax.rem(pair, NX)
    y, core = slab // 2, lax.rem(slab, 2)
    sibling_core = 1 - core

    def at_pair(dz, dx):
        return wrap(z, dz, NZ) * NX + wrap(x, dx, NX)

    def at_slab(dy, own_core=True):
        return wrap(y, dy, NY) * 2 + (core if own_core else sibling_core)

    device = {"sibling": (pair, at_slab(0, False))}
    for step in (2, 1, -1):
        device["x", step] = (at_pair(0, step), slab)
        device["z", step] = (at_pair(step, 0), slab)
        device["y", step] = (pair, at_slab(step))

    loads = [
        pltpu.make_async_copy(src, dst, load_sems.at[at])
        for at, (src, dst) in enumerate((
            (virt_hbm, virt_ref),
            (occ_hbm, occ_ref),
            (slab_hbm, slab_ref),
            (amps_hbm.at[:, core], amps),
            (ints_hbm.at[:, 0], ints),
            (amps_hbm.at[:, sibling_core], to_sibling),
        ))
    ]

    barrier = pltpu.get_barrier_semaphore()
    for to in device.values():
        pl.semaphore_signal(barrier, inc=1, device_id=to, device_id_type=pl.DeviceIdType.MESH)

    for load in loads:
        load.start()

    order, sent = {}, []

    def copy(group, src, dst, to):
        at = order.setdefault(group, len(order))
        return pltpu.make_async_remote_copy(
            src_ref=src, dst_ref=dst, send_sem=send_sems.at[0], recv_sem=recv_sems.at[at],
            device_id=device[to], device_id_type=pl.DeviceIdType.MESH,
        )

    def send(group, src, dst, to):
        copy(group, src, dst, to).start()
        sent.append(src.size // (16 * V))

    def arrive(group, like):
        copy(group, like, like, "sibling").wait_recv()

    for load in loads[:3]:
        load.wait()
    columns = virt_ref[...]
    for at in range(V // 128):
        lanes = jnp.broadcast_to(columns[:, at * 128 : (at + 1) * 128], (128, 128))
        row_labels[at * 128 : (at + 1) * 128, :] = lanes.T

    def pair_labels(tile):
        rows = row_labels[pl.ds(pl.multiple_of(tile * TILE, TILE), TILE), :]
        return jnp.concatenate([rows] * (V // 128), axis=1) ^ columns

    own_label = occ_ref[pair]
    amps_label = own_label ^ slab_ref[slab]
    sibling_label = own_label ^ slab_ref[at_slab(0, False)]

    loads[4].wait()
    wanted = pair_labels(slab) ^ own_label
    w = jnp.zeros((TILE, V), F32)
    for k in range(8):
        w = jnp.where(wanted == slab_ref[k], ints[k].astype(F32), w)
    w = w.astype(BF16).reshape(2, 2, 16, V)
    pair_w[pair] = w
    slab_w[slab] = w

    axes = (("x", "z", 0), ("z", "x", 1))

    def beside(axis, step, other=0):
        return at_pair(other, step) if axis == "x" else at_pair(step, other)

    def start_far(tag, buf, chunk):
        for axis, _, _ in axes:
            own = buf.at[pair, :, chunk]
            send((tag, str(chunk), 2), own, own, (axis, 2))

    def start_near(tag, buf, chunk):
        for step in NEAR:
            for axis, _, half in axes:
                own = buf.at[pair, half, chunk]
                send((tag, str(chunk), 1), own, own, (axis, step))

    def start_own(tag, buf, chunk):
        for step in NEAR:
            for axis, _, half in axes:
                own = buf.at[pair, 1 - half, chunk]
                send((tag, "own"), own, own, (axis, step))

    def turn_near(tag, buf, chunk):
        arrive((tag, str(chunk), 1), buf.at[pl.ds(0, 2), :, chunk])
        for step in NEAR:
            for axis, other, half in axes:
                piece = buf.at[beside(axis, -step), half, chunk]
                for way in NEAR:
                    send((tag, "near"), piece, piece, (other, way))
    def turn_far(tag, buf, chunk):
        arrive((tag, str(chunk), 2), buf.at[pl.ds(0, 2), :, chunk])
        for axis, other, half in axes:
            piece = buf.at[beside(axis, 2), :, chunk]
            for way in NEAR:
                send((tag, "far"), piece, piece, (other, way))
            piece = buf.at[beside(axis, 2), half, chunk]
            send((tag, "far"), piece, piece, (other, 2))

    def pair_own(tag, buf):
        arrive((tag, "own"), buf.at[pl.ds(0, 2)])

    def pair_near(tag, buf):
        arrive((tag, "near"), buf.at[pl.ds(0, 4)])

    def pair_far(tag, buf):
        arrive((tag, "far"), buf.at[pl.ds(0, 5)])

    def slab_start(tag, buf, steps):
        for step in steps:
            send((tag, step), buf.at[slab], buf.at[slab], ("y", step))

    def slab_over(tag, buf):
        send((tag, "sibling"), buf.at[slab], buf.at[slab], "sibling")
        for step in STEPS:
            piece = buf.at[at_slab(-step)]
            arrive((tag, step), piece)
            send((tag, "sibling"), piece, piece, "sibling")

    def slab_end(tag, buf):
        arrive((tag, "sibling"), buf.at[pl.ds(0, NY)])

    loads[5].wait()
    pl.semaphore_wait(barrier, len(device))
    for chunk in range(2):
        send(("merge", chunk), to_sibling.at[:, :, chunk], from_sibling.at[:, :, chunk], "sibling")

    whole = pl.ds(0, 2)
    start_far("pw", pair_w, 0)
    start_near("pw", pair_w, 0)
    start_far("pw", pair_w, 1)
    start_near("pw", pair_w, 1)
    slab_start("sw", slab_w, NEAR)

    loads[3].wait()
    def merged(at, chunk):
        labels = pair_labels(2 * at + core).reshape(2, 2, 16, V)[:, chunk]
        other = jnp.where(labels == sibling_label, from_sibling[at, :, chunk].astype(F32), 0.0)
        return jnp.where(labels == amps_label, amps[at, :, chunk].astype(F32), other).astype(BF16)

    for chunk in range(2):
        arrive(("merge", chunk), from_sibling.at[:, :, chunk])
        for at, step in enumerate(STEPS):
            part[at, :, chunk] = merged(wrap(y, step, NY), chunk)
            send(("ring", chunk), part.at[at, :, chunk], from_ring.at[at, :, chunk], ("y", step))
    slab_start("sw", slab_w, (2,))
    start_own("pw", pair_w, whole)

    def ring_end(chunk):
        total = merged(y, chunk)
        arrive(("ring", chunk), from_ring.at[:, :, chunk])
        for at in range(len(STEPS)):
            total = total + from_ring[at, :, chunk]
        pair_a[pair, :, chunk] = total
        slab_a[slab, :, chunk] = total

    turn_near("pw", pair_w, 0)
    turn_far("pw", pair_w, 0)
    turn_near("pw", pair_w, 1)
    turn_far("pw", pair_w, 1)
    ring_end(0)
    start_far("pa", pair_a, 0)
    start_near("pa", pair_a, 0)
    ring_end(1)
    start_far("pa", pair_a, 1)
    start_near("pa", pair_a, 1)
    start_own("pa", pair_a, 0)
    start_own("pa", pair_a, 1)
    slab_start("sa", slab_a, STEPS)
    turn_far("pa", pair_a, 0)
    turn_near("pa", pair_a, 0)
    slab_over("sw", slab_w)
    turn_far("pa", pair_a, 1)
    turn_near("pa", pair_a, 1)

    slab_over("sa", slab_a)
    pair_own("pw", pair_w)
    pair_near("pw", pair_w)
    pair_far("pw", pair_w)
    slab_end("sw", slab_w)
    slab_end("sa", slab_a)

    @pl.loop(0, 2)
    def _(at):
        half = NJ // 2
        rows = pair_w[pl.ds(at * half, half)].reshape(half * TILE, V)
        out_ref[pl.ds(at * half, half)] = times(rows, slab_a[...].reshape(V, V)).reshape(half, TILE, V)

    labels = pair_labels(slab) ^ own_label

    def second_term(group):
        rows = jnp.concatenate([pair_a[j].reshape(TILE, V) for j in group], axis=0)
        term = times(rows, slab_w[...].reshape(V, V))
        for at, j in enumerate(group):
            both = out_ref[j] + term[at * TILE : (at + 1) * TILE]
            out_ref[j] = jnp.where(labels == occ_ref[j], both, 0.0)

    pair_own("pa", pair_a)
    second_term([pair] + [beside(axis, step) for axis in ("x", "z") for step in STEPS])
    every_ref[...] = slab_w[...].reshape(V, V)
    labels_ref[...] = labels
    for at, j in enumerate(far_pieces(z, x)):
        late_ref[at : at + 1, :] = jnp.full((1, 128), occ_ref[j], jnp.int32)
    pair_near("pa", pair_a)
    for at, j in enumerate(far_pieces(z, x)):
        if at == 4:
            pair_far("pa", pair_a)
        rows_ref[at * TILE : (at + 1) * TILE, :] = pair_a[j].reshape(TILE, V)

    assert sum(sent) == N_SENT
    copy(("merge", 0), spent, spent, "sibling").wait_send()


def solution(mesh):
    placed = (P("pair", "slab", None, None), P(None, "pair", "slab", None), P(), P(), P())
    piece = (2, 2, 16, V)

    def local(amplitudes, integrals, occ_irrep, slab_irrep, virt_irrep):
        operands = (
            amplitudes.reshape(NY, 2, *piece), integrals, occ_irrep.reshape(NJ), slab_irrep, virt_irrep.reshape(1, V)
        )
        gathered = pl.pallas_call(
            kernel,
            out_shape=(
                jax.ShapeDtypeStruct((NJ, TILE, V), F32),
                jax.ShapeDtypeStruct((9 * TILE, V), BF16),
                jax.ShapeDtypeStruct((V, V), BF16),
                jax.ShapeDtypeStruct((TILE, V), jnp.int32),
                jax.ShapeDtypeStruct((16, 128), jnp.int32),
            ),
            in_specs=[pl.BlockSpec(memory_space=pltpu.HBM)] * 5,
            out_specs=[pl.BlockSpec(memory_space=pltpu.VMEM)] * 5,
            scratch_shapes=[
                pltpu.VMEM((NY, *piece), BF16),
                pltpu.VMEM((8, TILE, V), BF16),
                pltpu.SMEM((NJ,), jnp.int32),
                pltpu.SMEM((8,), jnp.int32),
                pltpu.VMEM((1, V), jnp.int32),
                pltpu.VMEM((V, 128), jnp.int32),
                pltpu.VMEM((NY, *piece), BF16),
                pltpu.VMEM((NY, *piece), BF16),
                pltpu.VMEM((3, *piece), BF16),
                pltpu.VMEM((3, *piece), BF16),
                pltpu.VMEM((NJ, *piece), BF16),
                pltpu.VMEM((NJ, *piece), BF16),
                pltpu.VMEM((NS, *piece), BF16),
                pltpu.VMEM((NS, *piece), BF16),
                pltpu.VMEM((N_SENT, 16, V), BF16),
                pltpu.SemaphoreType.DMA((6,)),
                pltpu.SemaphoreType.DMA((1,)),
                pltpu.SemaphoreType.DMA((N_SEMS,)),
            ],
            compiler_params=pltpu.CompilerParams(
                collective_id=0, has_side_effects=True, vmem_limit_bytes=32 * 1024 * 1024
            ),
        )(*(pltpu.with_memory_space_constraint(operand, pltpu.HBM) for operand in operands))
        residual = pl.pallas_call(
            finish,
            out_shape=jax.ShapeDtypeStruct((NJ, TILE, V), F32),
            in_specs=[pl.BlockSpec(memory_space=pltpu.VMEM)] * 5,
            out_specs=pl.BlockSpec(memory_space=pltpu.HBM),
            scratch_shapes=[pltpu.VMEM((9, TILE, V), F32), pltpu.SemaphoreType.DMA((2,))],
            compiler_params=pltpu.CompilerParams(vmem_limit_bytes=16 * 1024 * 1024),
        )(*gathered)
        return residual[None]

    return jax.shard_map(
        local, mesh=mesh, in_specs=placed, out_specs=P("pair", None, "slab", None), check_vma=False
    )
```

```python
import jax
import jax.numpy as jnp
from jax import lax
from jax.experimental import pallas as pl
from jax.experimental.pallas import tpu as pltpu
from jax.sharding import PartitionSpec as P

NX = NY = NZ = 4
NJ = 16
NS = 8
TILE = 64
V = 512
N_SEMS = 26
N_SENT = 204
NEAR = (1, -1)
STEPS = (1, -1, 2)
BF16 = jnp.bfloat16
F32 = jnp.float32


def wrap(at, step, size):
    return lax.rem(at + step + size, size)


def times(rows, every):
    return lax.dot_general(rows, every, (((1,), (1,)), ((), ())), preferred_element_type=F32)


def pieces_at(z, x, steps):
    return [wrap(z, dz, NZ) * NX + wrap(x, dx, NX) for dz, dx in steps]


def near_pieces(z, x):
    return pieces_at(z, x, [(0, 0)] + [(0, s) for s in STEPS] + [(s, 0) for s in STEPS])


def far_pieces(z, x):
    return pieces_at(z, x, [(a, b) for a in NEAR for b in NEAR] + [(2, s) for s in STEPS] + [(s, 2) for s in NEAR])


def finish(done_ref, rows_ref, every_ref, labels_ref, late_ref, out_hbm, last, sems):
    pair = lax.axis_index("pair")
    z, x = pair // NX, lax.rem(pair, NX)
    near, far = near_pieces(z, x), far_pieces(z, x)
    for j in near:
        pltpu.make_async_copy(done_ref.at[j], out_hbm.at[j], sems.at[0]).start()
    for first, after in ((0, 4), (4, 9)):
        term = times(rows_ref[first * TILE : after * TILE, :], every_ref[...])
        for at in range(first, after):
            kept = labels_ref[...] == jnp.concatenate([late_ref[at : at + 1, :]] * (V // 128), axis=1)
            both = done_ref[far[at]] + term[(at - first) * TILE : (at - first + 1) * TILE]
            last[at] = jnp.where(kept, both, 0.0)
            pltpu.make_async_copy(last.at[at], out_hbm.at[far[at]], sems.at[1]).start()
    many = done_ref.at[pl.ds(0, len(near))]
    pltpu.make_async_copy(many, out_hbm.at[pl.ds(0, len(near))], sems.at[0]).wait()
    pltpu.make_async_copy(last, out_hbm.at[pl.ds(0, len(far))], sems.at[1]).wait()


def kernel(
    amps_hbm, ints_hbm, occ_hbm, slab_hbm, virt_hbm, out_ref, rows_ref, every_ref, labels_ref, late_ref,
    amps, ints, occ_ref, slab_ref, virt_ref, row_labels, to_sibling, from_sibling, part, from_ring,
    pair_w, pair_a, slab_w, slab_a, spent, load_sems, send_sems, recv_sems,
):
    pair, slab = lax.axis_index("pair"), lax.axis_index("slab")
    z, x = pair // NX, lax.rem(pair, NX)
    y, core = slab // 2, lax.rem(slab, 2)
    sibling_core = 1 - core

    def at_pair(dz, dx):
        return wrap(z, dz, NZ) * NX + wrap(x, dx, NX)

    def at_slab(dy, own_core=True):
        return wrap(y, dy, NY) * 2 + (core if own_core else sibling_core)

    device = {"sibling": (pair, at_slab(0, False))}
    for step in (2, 1, -1):
        device["x", step] = (at_pair(0, step), slab)
        device["z", step] = (at_pair(step, 0), slab)
        device["y", step] = (pair, at_slab(step))

    loads = [
        pltpu.make_async_copy(src, dst, load_sems.at[at])
        for at, (src, dst) in enumerate((
            (virt_hbm, virt_ref),
            (occ_hbm, occ_ref),
            (slab_hbm, slab_ref),
            (amps_hbm.at[:, core], amps),
            (ints_hbm.at[:, 0], ints),
            (amps_hbm.at[:, sibling_core], to_sibling),
        ))
    ]

    barrier = pltpu.get_barrier_semaphore()
    for to in device.values():
        pl.semaphore_signal(barrier, inc=1, device_id=to, device_id_type=pl.DeviceIdType.MESH)

    for load in loads:
        load.start()

    order, sent = {}, []

    def copy(group, src, dst, to):
        at = order.setdefault(group, len(order))
        return pltpu.make_async_remote_copy(
            src_ref=src, dst_ref=dst, send_sem=send_sems.at[0], recv_sem=recv_sems.at[at],
            device_id=device[to], device_id_type=pl.DeviceIdType.MESH,
        )

    def send(group, src, dst, to):
        copy(group, src, dst, to).start()
        sent.append(src.size // (16 * V))

    def arrive(group, like):
        copy(group, like, like, "sibling").wait_recv()

    for load in loads[:3]:
        load.wait()
    columns = virt_ref[...]
    for at in range(V // 128):
        lanes = jnp.broadcast_to(columns[:, at * 128 : (at + 1) * 128], (128, 128))
        row_labels[at * 128 : (at + 1) * 128, :] = lanes.T

    def pair_labels(tile):
        rows = row_labels[pl.ds(pl.multiple_of(tile * TILE, TILE), TILE), :]
        return jnp.concatenate([rows] * (V // 128), axis=1) ^ columns

    own_label = occ_ref[pair]
    amps_label = own_label ^ slab_ref[slab]
    sibling_label = own_label ^ slab_ref[at_slab(0, False)]

    loads[4].wait()
    wanted = pair_labels(slab) ^ own_label
    w = jnp.zeros((TILE, V), F32)
    for k in range(8):
        w = jnp.where(wanted == slab_ref[k], ints[k].astype(F32), w)
    w = w.astype(BF16).reshape(2, 2, 16, V)
    pair_w[pair] = w
    slab_w[slab] = w

    axes = (("x", "z", 0), ("z", "x", 1))

    def beside(axis, step, other=0):
        return at_pair(other, step) if axis == "x" else at_pair(step, other)

    def start_far(tag, buf, chunk):
        for axis, _, _ in axes:
            own = buf.at[pair, :, chunk]
            send((tag, str(chunk), 2), own, own, (axis, 2))

    def start_near(tag, buf, chunk):
        for step in NEAR:
            for axis, _, half in axes:
                own = buf.at[pair, half, chunk]
                send((tag, str(chunk), 1), own, own, (axis, step))

    def start_own(tag, buf, chunk):
        for step in NEAR:
            for axis, _, half in axes:
                own = buf.at[pair, 1 - half, chunk]
                send((tag, "own"), own, own, (axis, step))

    def turn_near(tag, buf, chunk):
        arrive((tag, str(chunk), 1), buf.at[pl.ds(0, 2), :, chunk])
        for step in NEAR:
            for axis, other, half in axes:
                piece = buf.at[beside(axis, -step), half, chunk]
                for way in NEAR:
                    send((tag, "near"), piece, piece, (other, way))
    def turn_far(tag, buf, chunk):
        arrive((tag, str(chunk), 2), buf.at[pl.ds(0, 2), :, chunk])
        for axis, other, half in axes:
            piece = buf.at[beside(axis, 2), :, chunk]
            for way in NEAR:
                send((tag, "far"), piece, piece, (other, way))
            piece = buf.at[beside(axis, 2), half, chunk]
            send((tag, "far"), piece, piece, (other, 2))

    def pair_own(tag, buf):
        arrive((tag, "own"), buf.at[pl.ds(0, 2)])

    def pair_near(tag, buf):
        arrive((tag, "near"), buf.at[pl.ds(0, 4)])

    def pair_far(tag, buf):
        arrive((tag, "far"), buf.at[pl.ds(0, 5)])

    def slab_start(tag, buf, steps, chunk=slice(None)):
        own = buf.at[slab, :, chunk]
        for step in steps:
            send((tag, step), own, own, ("y", step))

    def slab_over(tag, buf):
        send((tag, "sibling"), buf.at[slab], buf.at[slab], "sibling")
        for step in STEPS:
            piece = buf.at[at_slab(-step)]
            arrive((tag, step), piece)
            send((tag, "sibling"), piece, piece, "sibling")

    def slab_end(tag, buf):
        arrive((tag, "sibling"), buf.at[pl.ds(0, NY)])

    loads[5].wait()
    pl.semaphore_wait(barrier, len(device))
    for chunk in range(2):
        send(("merge", chunk), to_sibling.at[:, :, chunk], from_sibling.at[:, :, chunk], "sibling")

    whole = pl.ds(0, 2)
    start_far("pw", pair_w, 0)
    start_near("pw", pair_w, 0)
    start_far("pw", pair_w, 1)
    start_near("pw", pair_w, 1)
    slab_start("sw", slab_w, NEAR)

    loads[3].wait()
    def merged(at, chunk):
        labels = pair_labels(2 * at + core).reshape(2, 2, 16, V)[:, chunk]
        other = jnp.where(labels == sibling_label, from_sibling[at, :, chunk].astype(F32), 0.0)
        return jnp.where(labels == amps_label, amps[at, :, chunk].astype(F32), other).astype(BF16)

    for chunk in range(2):
        arrive(("merge", chunk), from_sibling.at[:, :, chunk])
        for at, step in enumerate(STEPS):
            part[at, :, chunk] = merged(wrap(y, step, NY), chunk)
            send(("ring", chunk), part.at[at, :, chunk], from_ring.at[at, :, chunk], ("y", step))
    slab_start("sw", slab_w, (2,))
    start_own("pw", pair_w, whole)

    def ring_end(chunk):
        total = merged(y, chunk)
        arrive(("ring", chunk), from_ring.at[:, :, chunk])
        for at in range(len(STEPS)):
            total = total + from_ring[at, :, chunk]
        pair_a[pair, :, chunk] = total
        slab_a[slab, :, chunk] = total

    turn_near("pw", pair_w, 0)
    turn_far("pw", pair_w, 0)
    turn_near("pw", pair_w, 1)
    turn_far("pw", pair_w, 1)
    ring_end(0)
    start_far("pa", pair_a, 0)
    start_near("pa", pair_a, 0)
    slab_start("sa", slab_a, STEPS, 0)
    ring_end(1)
    start_far("pa", pair_a, 1)
    start_near("pa", pair_a, 1)
    slab_start("sa", slab_a, STEPS, 1)
    start_own("pa", pair_a, 0)
    start_own("pa", pair_a, 1)
    turn_far("pa", pair_a, 0)
    turn_near("pa", pair_a, 0)
    slab_over("sw", slab_w)
    turn_far("pa", pair_a, 1)
    turn_near("pa", pair_a, 1)

    slab_over("sa", slab_a)
    pair_own("pw", pair_w)
    pair_near("pw", pair_w)
    pair_far("pw", pair_w)
    slab_end("sw", slab_w)
    slab_end("sa", slab_a)

    @pl.loop(0, 2)
    def _(at):
        half = NJ // 2
        rows = pair_w[pl.ds(at * half, half)].reshape(half * TILE, V)
        out_ref[pl.ds(at * half, half)] = times(rows, slab_a[...].reshape(V, V)).reshape(half, TILE, V)

    labels = pair_labels(slab) ^ own_label

    def second_term(group):
        rows = jnp.concatenate([pair_a[j].reshape(TILE, V) for j in group], axis=0)
        term = times(rows, slab_w[...].reshape(V, V))
        for at, j in enumerate(group):
            both = out_ref[j] + term[at * TILE : (at + 1) * TILE]
            out_ref[j] = jnp.where(labels == occ_ref[j], both, 0.0)

    pair_own("pa", pair_a)
    second_term([pair] + [beside(axis, step) for axis in ("x", "z") for step in STEPS])
    every_ref[...] = slab_w[...].reshape(V, V)
    labels_ref[...] = labels
    for at, j in enumerate(far_pieces(z, x)):
        late_ref[at : at + 1, :] = jnp.full((1, 128), occ_ref[j], jnp.int32)
    pair_near("pa", pair_a)
    for at, j in enumerate(far_pieces(z, x)):
        if at == 4:
            pair_far("pa", pair_a)
        rows_ref[at * TILE : (at + 1) * TILE, :] = pair_a[j].reshape(TILE, V)

    assert sum(sent) == N_SENT
    copy(("merge", 0), spent, spent, "sibling").wait_send()


def solution(mesh):
    placed = (P("pair", "slab", None, None), P(None, "pair", "slab", None), P(), P(), P())
    piece = (2, 2, 16, V)

    def local(amplitudes, integrals, occ_irrep, slab_irrep, virt_irrep):
        operands = (
            amplitudes.reshape(NY, 2, *piece), integrals, occ_irrep.reshape(NJ), slab_irrep, virt_irrep.reshape(1, V)
        )
        gathered = pl.pallas_call(
            kernel,
            out_shape=(
                jax.ShapeDtypeStruct((NJ, TILE, V), F32),
                jax.ShapeDtypeStruct((9 * TILE, V), BF16),
                jax.ShapeDtypeStruct((V, V), BF16),
                jax.ShapeDtypeStruct((TILE, V), jnp.int32),
                jax.ShapeDtypeStruct((16, 128), jnp.int32),
            ),
            in_specs=[pl.BlockSpec(memory_space=pltpu.HBM)] * 5,
            out_specs=[pl.BlockSpec(memory_space=pltpu.VMEM)] * 5,
            scratch_shapes=[
                pltpu.VMEM((NY, *piece), BF16),
                pltpu.VMEM((8, TILE, V), BF16),
                pltpu.SMEM((NJ,), jnp.int32),
                pltpu.SMEM((8,), jnp.int32),
                pltpu.VMEM((1, V), jnp.int32),
                pltpu.VMEM((V, 128), jnp.int32),
                pltpu.VMEM((NY, *piece), BF16),
                pltpu.VMEM((NY, *piece), BF16),
                pltpu.VMEM((3, *piece), BF16),
                pltpu.VMEM((3, *piece), BF16),
                pltpu.VMEM((NJ, *piece), BF16),
                pltpu.VMEM((NJ, *piece), BF16),
                pltpu.VMEM((NS, *piece), BF16),
                pltpu.VMEM((NS, *piece), BF16),
                pltpu.VMEM((N_SENT, 16, V), BF16),
                pltpu.SemaphoreType.DMA((6,)),
                pltpu.SemaphoreType.DMA((1,)),
                pltpu.SemaphoreType.DMA((N_SEMS,)),
            ],
            compiler_params=pltpu.CompilerParams(
                collective_id=0, has_side_effects=True, vmem_limit_bytes=32 * 1024 * 1024
            ),
        )(*(pltpu.with_memory_space_constraint(operand, pltpu.HBM) for operand in operands))
        residual = pl.pallas_call(
            finish,
            out_shape=jax.ShapeDtypeStruct((NJ, TILE, V), F32),
            in_specs=[pl.BlockSpec(memory_space=pltpu.VMEM)] * 5,
            out_specs=pl.BlockSpec(memory_space=pltpu.HBM),
            scratch_shapes=[pltpu.VMEM((9, TILE, V), F32), pltpu.SemaphoreType.DMA((2,))],
            compiler_params=pltpu.CompilerParams(vmem_limit_bytes=16 * 1024 * 1024),
        )(*gathered)
        return residual[None]

    return jax.shard_map(
        local, mesh=mesh, in_specs=placed, out_specs=P("pair", None, "slab", None), check_vma=False
    )
```

```python
import jax
import jax.numpy as jnp
from jax import lax
from jax.experimental import pallas as pl
from jax.experimental.pallas import tpu as pltpu
from jax.sharding import PartitionSpec as P

NX = NY = NZ = 4
NJ = 16
NS = 8
TILE = 64
V = 512
N_SEMS = 26
N_SENT = 204
NEAR = (1, -1)
STEPS = (1, -1, 2)
BF16 = jnp.bfloat16
F32 = jnp.float32


def wrap(at, step, size):
    return lax.rem(at + step + size, size)


def times(rows, every):
    return lax.dot_general(rows, every, (((1,), (1,)), ((), ())), preferred_element_type=F32)


def pieces_at(z, x, steps):
    return [wrap(z, dz, NZ) * NX + wrap(x, dx, NX) for dz, dx in steps]


def near_pieces(z, x):
    return pieces_at(z, x, [(0, 0)] + [(0, s) for s in STEPS] + [(s, 0) for s in STEPS])


def far_pieces(z, x):
    return pieces_at(z, x, [(a, b) for a in NEAR for b in NEAR] + [(2, s) for s in STEPS] + [(s, 2) for s in NEAR])


def finish(done_ref, rows_ref, every_ref, labels_ref, late_ref, out_hbm, last, sems):
    pair = lax.axis_index("pair")
    z, x = pair // NX, lax.rem(pair, NX)
    near, far = near_pieces(z, x), far_pieces(z, x)
    for j in near:
        pltpu.make_async_copy(done_ref.at[j], out_hbm.at[j], sems.at[0]).start()
    for first, after in ((0, 4), (4, 9)):
        term = times(rows_ref[first * TILE : after * TILE, :], every_ref[...])
        for at in range(first, after):
            kept = labels_ref[...] == jnp.concatenate([late_ref[at : at + 1, :]] * (V // 128), axis=1)
            both = done_ref[far[at]] + term[(at - first) * TILE : (at - first + 1) * TILE]
            last[at] = jnp.where(kept, both, 0.0)
            pltpu.make_async_copy(last.at[at], out_hbm.at[far[at]], sems.at[1]).start()
    many = done_ref.at[pl.ds(0, len(near))]
    pltpu.make_async_copy(many, out_hbm.at[pl.ds(0, len(near))], sems.at[0]).wait()
    pltpu.make_async_copy(last, out_hbm.at[pl.ds(0, len(far))], sems.at[1]).wait()


def kernel(
    amps_hbm, ints_hbm, occ_hbm, slab_hbm, virt_hbm, out_ref, rows_ref, every_ref, labels_ref, late_ref,
    amps, ints, occ_ref, slab_ref, virt_ref, row_labels, to_sibling, from_sibling, part, from_ring,
    pair_w, pair_a, slab_w, slab_a, spent, load_sems, send_sems, recv_sems,
):
    pair, slab = lax.axis_index("pair"), lax.axis_index("slab")
    z, x = pair // NX, lax.rem(pair, NX)
    y, core = slab // 2, lax.rem(slab, 2)
    sibling_core = 1 - core

    def at_pair(dz, dx):
        return wrap(z, dz, NZ) * NX + wrap(x, dx, NX)

    def at_slab(dy, own_core=True):
        return wrap(y, dy, NY) * 2 + (core if own_core else sibling_core)

    device = {"sibling": (pair, at_slab(0, False))}
    for step in (2, 1, -1):
        device["x", step] = (at_pair(0, step), slab)
        device["z", step] = (at_pair(step, 0), slab)
        device["y", step] = (pair, at_slab(step))

    loads = [
        pltpu.make_async_copy(src, dst, load_sems.at[at])
        for at, (src, dst) in enumerate((
            (virt_hbm, virt_ref),
            (occ_hbm, occ_ref),
            (slab_hbm, slab_ref),
            (amps_hbm.at[:, core], amps),
            (ints_hbm.at[:, 0], ints),
            (amps_hbm.at[:, sibling_core], to_sibling),
        ))
    ]

    barrier = pltpu.get_barrier_semaphore()
    for to in device.values():
        pl.semaphore_signal(barrier, inc=1, device_id=to, device_id_type=pl.DeviceIdType.MESH)

    for load in loads:
        load.start()

    order, sent = {}, []

    def copy(group, src, dst, to):
        at = order.setdefault(group, len(order))
        return pltpu.make_async_remote_copy(
            src_ref=src, dst_ref=dst, send_sem=send_sems.at[0], recv_sem=recv_sems.at[at],
            device_id=device[to], device_id_type=pl.DeviceIdType.MESH,
        )

    def send(group, src, dst, to):
        copy(group, src, dst, to).start()
        sent.append(src.size // (16 * V))

    def arrive(group, like):
        copy(group, like, like, "sibling").wait_recv()

    for load in loads[:3]:
        load.wait()
    columns = virt_ref[...]
    for at in range(V // 128):
        lanes = jnp.broadcast_to(columns[:, at * 128 : (at + 1) * 128], (128, 128))
        row_labels[at * 128 : (at + 1) * 128, :] = lanes.T

    def pair_labels(tile):
        rows = row_labels[pl.ds(pl.multiple_of(tile * TILE, TILE), TILE), :]
        return jnp.concatenate([rows] * (V // 128), axis=1) ^ columns

    own_label = occ_ref[pair]
    amps_label = own_label ^ slab_ref[slab]

    def allowed(rows, of_core):
        for at in range(NY):
            labels = pair_labels(2 * at + of_core).reshape(2, 2, 16, V)
            rows[at] = jnp.where(labels == amps_label, rows[at].astype(F32), 0.0).astype(BF16)

    loads[4].wait()
    wanted = pair_labels(slab) ^ own_label
    w = jnp.zeros((TILE, V), F32)
    for k in range(8):
        w = jnp.where(wanted == slab_ref[k], ints[k].astype(F32), w)
    w = w.astype(BF16).reshape(2, 2, 16, V)
    pair_w[pair] = w
    slab_w[slab] = w

    axes = (("x", "z", 0), ("z", "x", 1))

    def beside(axis, step, other=0):
        return at_pair(other, step) if axis == "x" else at_pair(step, other)

    def start_far(tag, buf, chunk):
        for axis, _, _ in axes:
            own = buf.at[pair, :, chunk]
            send((tag, str(chunk), 2), own, own, (axis, 2))

    def start_near(tag, buf, chunk):
        for step in NEAR:
            for axis, _, half in axes:
                own = buf.at[pair, half, chunk]
                send((tag, str(chunk), 1), own, own, (axis, step))

    def start_own(tag, buf, chunk):
        for step in NEAR:
            for axis, _, half in axes:
                own = buf.at[pair, 1 - half, chunk]
                send((tag, "own"), own, own, (axis, step))

    def turn_near(tag, buf, chunk):
        arrive((tag, str(chunk), 1), buf.at[pl.ds(0, 2), :, chunk])
        for step in NEAR:
            for axis, other, half in axes:
                piece = buf.at[beside(axis, -step), half, chunk]
                for way in NEAR:
                    send((tag, "near"), piece, piece, (other, way))
    def turn_far(tag, buf, chunk):
        arrive((tag, str(chunk), 2), buf.at[pl.ds(0, 2), :, chunk])
        for axis, other, half in axes:
            piece = buf.at[beside(axis, 2), :, chunk]
            for way in NEAR:
                send((tag, "far"), piece, piece, (other, way))
            piece = buf.at[beside(axis, 2), half, chunk]
            send((tag, "far"), piece, piece, (other, 2))

    def pair_own(tag, buf):
        arrive((tag, "own"), buf.at[pl.ds(0, 2)])

    def pair_near(tag, buf):
        arrive((tag, "near"), buf.at[pl.ds(0, 4)])

    def pair_far(tag, buf):
        arrive((tag, "far"), buf.at[pl.ds(0, 5)])

    def slab_start(tag, buf, steps):
        for step in steps:
            send((tag, step), buf.at[slab], buf.at[slab], ("y", step))

    def slab_over(tag, buf):
        send((tag, "sibling"), buf.at[slab], buf.at[slab], "sibling")
        for step in STEPS:
            piece = buf.at[at_slab(-step)]
            arrive((tag, step), piece)
            send((tag, "sibling"), piece, piece, "sibling")

    def slab_end(tag, buf):
        arrive((tag, "sibling"), buf.at[pl.ds(0, NY)])

    loads[5].wait()
    allowed(to_sibling, sibling_core)
    loads[3].wait()
    allowed(amps, core)
    pl.semaphore_wait(barrier, len(device))
    for chunk in range(2):
        send(("merge", chunk), to_sibling.at[:, :, chunk], from_sibling.at[:, :, chunk], "sibling")

    whole = pl.ds(0, 2)
    start_far("pw", pair_w, 0)
    start_near("pw", pair_w, 0)
    start_far("pw", pair_w, 1)
    start_near("pw", pair_w, 1)
    slab_start("sw", slab_w, NEAR)

    def merged(at, chunk):
        return amps[at, :, chunk] + from_sibling[at, :, chunk]

    for chunk in range(2):
        arrive(("merge", chunk), from_sibling.at[:, :, chunk])
        for at, step in enumerate((2, 1, -1)):
            part[at, :, chunk] = merged(wrap(y, step, NY), chunk)
            send(("ring", chunk), part.at[at, :, chunk], from_ring.at[at, :, chunk], ("y", step))
    slab_start("sw", slab_w, (2,))
    start_own("pw", pair_w, whole)

    def ring_end(chunk):
        total = merged(y, chunk)
        arrive(("ring", chunk), from_ring.at[:, :, chunk])
        for at in range(len(STEPS)):
            total = total + from_ring[at, :, chunk]
        pair_a[pair, :, chunk] = total
        slab_a[slab, :, chunk] = total

    turn_near("pw", pair_w, 0)
    turn_far("pw", pair_w, 0)
    turn_near("pw", pair_w, 1)
    turn_far("pw", pair_w, 1)
    ring_end(0)
    start_far("pa", pair_a, 0)
    start_near("pa", pair_a, 0)
    ring_end(1)
    start_far("pa", pair_a, 1)
    start_near("pa", pair_a, 1)
    start_own("pa", pair_a, 0)
    start_own("pa", pair_a, 1)
    slab_start("sa", slab_a, STEPS)
    turn_far("pa", pair_a, 0)
    turn_near("pa", pair_a, 0)
    slab_over("sw", slab_w)
    turn_far("pa", pair_a, 1)
    turn_near("pa", pair_a, 1)

    slab_over("sa", slab_a)
    pair_own("pw", pair_w)
    pair_near("pw", pair_w)
    pair_far("pw", pair_w)
    slab_end("sw", slab_w)
    slab_end("sa", slab_a)

    @pl.loop(0, 2)
    def _(at):
        half = NJ // 2
        rows = pair_w[pl.ds(at * half, half)].reshape(half * TILE, V)
        out_ref[pl.ds(at * half, half)] = times(rows, slab_a[...].reshape(V, V)).reshape(half, TILE, V)

    labels = pair_labels(slab) ^ own_label

    def second_term(group):
        rows = jnp.concatenate([pair_a[j].reshape(TILE, V) for j in group], axis=0)
        term = times(rows, slab_w[...].reshape(V, V))
        for at, j in enumerate(group):
            both = out_ref[j] + term[at * TILE : (at + 1) * TILE]
            out_ref[j] = jnp.where(labels == occ_ref[j], both, 0.0)

    pair_own("pa", pair_a)
    second_term([pair] + [beside(axis, step) for axis in ("x", "z") for step in STEPS])
    every_ref[...] = slab_w[...].reshape(V, V)
    labels_ref[...] = labels
    for at, j in enumerate(far_pieces(z, x)):
        late_ref[at : at + 1, :] = jnp.full((1, 128), occ_ref[j], jnp.int32)
    pair_near("pa", pair_a)
    for at, j in enumerate(far_pieces(z, x)):
        if at == 4:
            pair_far("pa", pair_a)
        rows_ref[at * TILE : (at + 1) * TILE, :] = pair_a[j].reshape(TILE, V)

    assert sum(sent) == N_SENT
    copy(("merge", 0), spent, spent, "sibling").wait_send()


def solution(mesh):
    placed = (P("pair", "slab", None, None), P(None, "pair", "slab", None), P(), P(), P())
    piece = (2, 2, 16, V)

    def local(amplitudes, integrals, occ_irrep, slab_irrep, virt_irrep):
        operands = (
            amplitudes.reshape(NY, 2, *piece), integrals, occ_irrep.reshape(NJ), slab_irrep, virt_irrep.reshape(1, V)
        )
        gathered = pl.pallas_call(
            kernel,
            out_shape=(
                jax.ShapeDtypeStruct((NJ, TILE, V), F32),
                jax.ShapeDtypeStruct((9 * TILE, V), BF16),
                jax.ShapeDtypeStruct((V, V), BF16),
                jax.ShapeDtypeStruct((TILE, V), jnp.int32),
                jax.ShapeDtypeStruct((16, 128), jnp.int32),
            ),
            in_specs=[pl.BlockSpec(memory_space=pltpu.HBM)] * 5,
            out_specs=[pl.BlockSpec(memory_space=pltpu.VMEM)] * 5,
            scratch_shapes=[
                pltpu.VMEM((NY, *piece), BF16),
                pltpu.VMEM((8, TILE, V), BF16),
                pltpu.SMEM((NJ,), jnp.int32),
                pltpu.SMEM((8,), jnp.int32),
                pltpu.VMEM((1, V), jnp.int32),
                pltpu.VMEM((V, 128), jnp.int32),
                pltpu.VMEM((NY, *piece), BF16),
                pltpu.VMEM((NY, *piece), BF16),
                pltpu.VMEM((3, *piece), BF16),
                pltpu.VMEM((3, *piece), BF16),
                pltpu.VMEM((NJ, *piece), BF16),
                pltpu.VMEM((NJ, *piece), BF16),
                pltpu.VMEM((NS, *piece), BF16),
                pltpu.VMEM((NS, *piece), BF16),
                pltpu.VMEM((N_SENT, 16, V), BF16),
                pltpu.SemaphoreType.DMA((6,)),
                pltpu.SemaphoreType.DMA((1,)),
                pltpu.SemaphoreType.DMA((N_SEMS,)),
            ],
            compiler_params=pltpu.CompilerParams(
                collective_id=0, has_side_effects=True, vmem_limit_bytes=32 * 1024 * 1024
            ),
        )(*(pltpu.with_memory_space_constraint(operand, pltpu.HBM) for operand in operands))
        residual = pl.pallas_call(
            finish,
            out_shape=jax.ShapeDtypeStruct((NJ, TILE, V), F32),
            in_specs=[pl.BlockSpec(memory_space=pltpu.VMEM)] * 5,
            out_specs=pl.BlockSpec(memory_space=pltpu.HBM),
            scratch_shapes=[pltpu.VMEM((9, TILE, V), F32), pltpu.SemaphoreType.DMA((2,))],
            compiler_params=pltpu.CompilerParams(vmem_limit_bytes=16 * 1024 * 1024),
        )(*gathered)
        return residual[None]

    return jax.shard_map(
        local, mesh=mesh, in_specs=placed, out_specs=P("pair", None, "slab", None), check_vma=False
    )
```

```python
import jax
import jax.numpy as jnp
from jax import lax
from jax.experimental import pallas as pl
from jax.experimental.pallas import tpu as pltpu
from jax.sharding import PartitionSpec as P

NX = NY = NZ = 4
NJ = 16
NS = 8
TILE = 64
V = 512
N_SEMS = 22
N_SENT = 204
NEAR = (1, -1)
STEPS = (1, -1, 2)
BF16 = jnp.bfloat16
F32 = jnp.float32


def wrap(at, step, size):
    return lax.rem(at + step + size, size)


def times(rows, every):
    return lax.dot_general(rows, every, (((1,), (1,)), ((), ())), preferred_element_type=F32)


def pieces_at(z, x, steps):
    return [wrap(z, dz, NZ) * NX + wrap(x, dx, NX) for dz, dx in steps]


def near_pieces(z, x):
    return pieces_at(z, x, [(0, 0)] + [(0, s) for s in STEPS] + [(s, 0) for s in STEPS])


def far_pieces(z, x):
    return pieces_at(z, x, [(a, b) for a in NEAR for b in NEAR] + [(2, s) for s in STEPS] + [(s, 2) for s in NEAR])


def finish(done_ref, rows_ref, every_ref, labels_ref, late_ref, out_hbm, last, sems):
    pair = lax.axis_index("pair")
    z, x = pair // NX, lax.rem(pair, NX)
    near, far = near_pieces(z, x), far_pieces(z, x)
    for j in near:
        pltpu.make_async_copy(done_ref.at[j], out_hbm.at[j], sems.at[0]).start()
    for first, after in ((0, 4), (4, 9)):
        term = times(rows_ref[first * TILE : after * TILE, :], every_ref[...])
        for at in range(first, after):
            kept = labels_ref[...] == jnp.concatenate([late_ref[at : at + 1, :]] * (V // 128), axis=1)
            both = done_ref[far[at]] + term[(at - first) * TILE : (at - first + 1) * TILE]
            last[at] = jnp.where(kept, both, 0.0)
            pltpu.make_async_copy(last.at[at], out_hbm.at[far[at]], sems.at[1]).start()
    many = done_ref.at[pl.ds(0, len(near))]
    pltpu.make_async_copy(many, out_hbm.at[pl.ds(0, len(near))], sems.at[0]).wait()
    pltpu.make_async_copy(last, out_hbm.at[pl.ds(0, len(far))], sems.at[1]).wait()


def kernel(
    amps_hbm, ints_hbm, occ_hbm, slab_hbm, virt_hbm, out_ref, rows_ref, every_ref, labels_ref, late_ref,
    amps, ints, occ_ref, slab_ref, virt_ref, row_labels, to_sibling, from_sibling, part, from_ring,
    pair_w, pair_a, slab_w, slab_a, spent, load_sems, send_sems, recv_sems,
):
    pair, slab = lax.axis_index("pair"), lax.axis_index("slab")
    z, x = pair // NX, lax.rem(pair, NX)
    y, core = slab // 2, lax.rem(slab, 2)
    sibling_core = 1 - core

    def at_pair(dz, dx):
        return wrap(z, dz, NZ) * NX + wrap(x, dx, NX)

    def at_slab(dy, own_core=True):
        return wrap(y, dy, NY) * 2 + (core if own_core else sibling_core)

    device = {"sibling": (pair, at_slab(0, False))}
    for step in (2, 1, -1):
        device["x", step] = (at_pair(0, step), slab)
        device["z", step] = (at_pair(step, 0), slab)
        device["y", step] = (pair, at_slab(step))

    loads = [
        pltpu.make_async_copy(src, dst, load_sems.at[at])
        for at, (src, dst) in enumerate((
            (virt_hbm, virt_ref),
            (occ_hbm, occ_ref),
            (slab_hbm, slab_ref),
            (amps_hbm.at[:, core], amps),
            (ints_hbm.at[:, 0], ints),
            (amps_hbm.at[:, sibling_core], to_sibling),
        ))
    ]

    barrier = pltpu.get_barrier_semaphore()
    for to in device.values():
        pl.semaphore_signal(barrier, inc=1, device_id=to, device_id_type=pl.DeviceIdType.MESH)

    for load in loads:
        load.start()

    order, sent = {}, []

    def copy(group, src, dst, to):
        at = order.setdefault(group, len(order))
        return pltpu.make_async_remote_copy(
            src_ref=src, dst_ref=dst, send_sem=send_sems.at[0], recv_sem=recv_sems.at[at],
            device_id=device[to], device_id_type=pl.DeviceIdType.MESH,
        )

    def send(group, src, dst, to):
        copy(group, src, dst, to).start()
        sent.append(src.size // (16 * V))

    def arrive(group, like):
        copy(group, like, like, "sibling").wait_recv()

    for load in loads[:3]:
        load.wait()
    columns = virt_ref[...]
    for at in range(V // 128):
        lanes = jnp.broadcast_to(columns[:, at * 128 : (at + 1) * 128], (128, 128))
        row_labels[at * 128 : (at + 1) * 128, :] = lanes.T

    def pair_labels(tile):
        rows = row_labels[pl.ds(pl.multiple_of(tile * TILE, TILE), TILE), :]
        return jnp.concatenate([rows] * (V // 128), axis=1) ^ columns

    own_label = occ_ref[pair]
    amps_label = own_label ^ slab_ref[slab]
    sibling_label = own_label ^ slab_ref[at_slab(0, False)]

    loads[4].wait()
    wanted = pair_labels(slab) ^ own_label
    w = jnp.zeros((TILE, V), F32)
    for k in range(8):
        w = jnp.where(wanted == slab_ref[k], ints[k].astype(F32), w)
    w = w.astype(BF16).reshape(2, 2, 16, V)
    pair_w[pair] = w
    slab_w[slab] = w

    axes = (("x", "z", 0), ("z", "x", 1))

    def beside(axis, step, other=0):
        return at_pair(other, step) if axis == "x" else at_pair(step, other)

    def start_far(tag, buf, chunk):
        for axis, _, _ in axes:
            own = buf.at[pair, :, chunk]
            send((tag, str(chunk), 2), own, own, (axis, 2))

    def start_near(tag, buf, chunk):
        for step in NEAR:
            for axis, _, half in axes:
                own = buf.at[pair, half, chunk]
                send((tag, str(chunk), 1), own, own, (axis, step))

    def start_own(tag, buf, chunk):
        for step in NEAR:
            for axis, _, half in axes:
                own = buf.at[pair, 1 - half, chunk]
                send((tag, "own"), own, own, (axis, step))

    def turn_near(tag, buf, chunk):
        arrive((tag, str(chunk), 1), buf.at[pl.ds(0, 2), :, chunk])
        for step in NEAR:
            for axis, other, half in axes:
                piece = buf.at[beside(axis, -step), half, chunk]
                for way in NEAR:
                    send((tag, "near"), piece, piece, (other, way))
    def turn_far(tag, buf, chunk):
        arrive((tag, str(chunk), 2), buf.at[pl.ds(0, 2), :, chunk])
        for axis, other, half in axes:
            piece = buf.at[beside(axis, 2), :, chunk]
            for way in NEAR:
                send((tag, "far"), piece, piece, (other, way))
            piece = buf.at[beside(axis, 2), half, chunk]
            send((tag, "far"), piece, piece, (other, 2))

    def pair_own(tag, buf):
        arrive((tag, "own"), buf.at[pl.ds(0, 2)])

    def pair_near(tag, buf):
        arrive((tag, "near"), buf.at[pl.ds(0, 4)])

    def pair_far(tag, buf):
        arrive((tag, "far"), buf.at[pl.ds(0, 5)])

    def slab_start(tag, buf, steps):
        for step in steps:
            send((tag, "y"), buf.at[slab], buf.at[slab], ("y", step))

    def slab_over(tag, buf):
        send((tag, "sibling"), buf.at[slab], buf.at[slab], "sibling")
        arrive((tag, "y"), buf.at[pl.ds(0, len(STEPS))])
        for step in STEPS:
            piece = buf.at[at_slab(-step)]
            send((tag, "sibling"), piece, piece, "sibling")

    def slab_end(tag, buf):
        arrive((tag, "sibling"), buf.at[pl.ds(0, NY)])

    loads[5].wait()
    pl.semaphore_wait(barrier, len(device))
    for chunk in range(2):
        send(("merge", chunk), to_sibling.at[:, :, chunk], from_sibling.at[:, :, chunk], "sibling")

    whole = pl.ds(0, 2)
    start_far("pw", pair_w, 0)
    start_near("pw", pair_w, 0)
    start_far("pw", pair_w, 1)
    start_near("pw", pair_w, 1)
    slab_start("sw", slab_w, NEAR)

    loads[3].wait()
    def merged(at, chunk):
        labels = pair_labels(2 * at + core).reshape(2, 2, 16, V)[:, chunk]
        other = jnp.where(labels == sibling_label, from_sibling[at, :, chunk].astype(F32), 0.0)
        return jnp.where(labels == amps_label, amps[at, :, chunk].astype(F32), other).astype(BF16)

    for chunk in range(2):
        arrive(("merge", chunk), from_sibling.at[:, :, chunk])
        for at, step in enumerate(STEPS):
            part[at, :, chunk] = merged(wrap(y, step, NY), chunk)
            send(("ring", chunk), part.at[at, :, chunk], from_ring.at[at, :, chunk], ("y", step))
    slab_start("sw", slab_w, (2,))
    start_own("pw", pair_w, whole)

    def ring_end(chunk):
        total = merged(y, chunk)
        arrive(("ring", chunk), from_ring.at[:, :, chunk])
        for at in range(len(STEPS)):
            total = total + from_ring[at, :, chunk]
        pair_a[pair, :, chunk] = total
        slab_a[slab, :, chunk] = total

    turn_near("pw", pair_w, 0)
    turn_far("pw", pair_w, 0)
    turn_near("pw", pair_w, 1)
    turn_far("pw", pair_w, 1)
    ring_end(0)
    start_far("pa", pair_a, 0)
    start_near("pa", pair_a, 0)
    ring_end(1)
    start_far("pa", pair_a, 1)
    start_near("pa", pair_a, 1)
    start_own("pa", pair_a, 0)
    start_own("pa", pair_a, 1)
    slab_start("sa", slab_a, STEPS)
    turn_far("pa", pair_a, 0)
    turn_near("pa", pair_a, 0)
    slab_over("sw", slab_w)
    turn_far("pa", pair_a, 1)
    turn_near("pa", pair_a, 1)

    slab_over("sa", slab_a)
    pair_own("pw", pair_w)
    pair_near("pw", pair_w)
    pair_far("pw", pair_w)
    slab_end("sw", slab_w)
    slab_end("sa", slab_a)

    @pl.loop(0, 2)
    def _(at):
        half = NJ // 2
        rows = pair_w[pl.ds(at * half, half)].reshape(half * TILE, V)
        out_ref[pl.ds(at * half, half)] = times(rows, slab_a[...].reshape(V, V)).reshape(half, TILE, V)

    labels = pair_labels(slab) ^ own_label

    def second_term(group):
        rows = jnp.concatenate([pair_a[j].reshape(TILE, V) for j in group], axis=0)
        term = times(rows, slab_w[...].reshape(V, V))
        for at, j in enumerate(group):
            both = out_ref[j] + term[at * TILE : (at + 1) * TILE]
            out_ref[j] = jnp.where(labels == occ_ref[j], both, 0.0)

    pair_own("pa", pair_a)
    second_term([pair] + [beside(axis, step) for axis in ("x", "z") for step in STEPS])
    every_ref[...] = slab_w[...].reshape(V, V)
    labels_ref[...] = labels
    for at, j in enumerate(far_pieces(z, x)):
        late_ref[at : at + 1, :] = jnp.full((1, 128), occ_ref[j], jnp.int32)
    pair_near("pa", pair_a)
    for at, j in enumerate(far_pieces(z, x)):
        if at == 4:
            pair_far("pa", pair_a)
        rows_ref[at * TILE : (at + 1) * TILE, :] = pair_a[j].reshape(TILE, V)

    assert sum(sent) == N_SENT
    copy(("merge", 0), spent, spent, "sibling").wait_send()


def solution(mesh):
    placed = (P("pair", "slab", None, None), P(None, "pair", "slab", None), P(), P(), P())
    piece = (2, 2, 16, V)

    def local(amplitudes, integrals, occ_irrep, slab_irrep, virt_irrep):
        operands = (
            amplitudes.reshape(NY, 2, *piece), integrals, occ_irrep.reshape(NJ), slab_irrep, virt_irrep.reshape(1, V)
        )
        gathered = pl.pallas_call(
            kernel,
            out_shape=(
                jax.ShapeDtypeStruct((NJ, TILE, V), F32),
                jax.ShapeDtypeStruct((9 * TILE, V), BF16),
                jax.ShapeDtypeStruct((V, V), BF16),
                jax.ShapeDtypeStruct((TILE, V), jnp.int32),
                jax.ShapeDtypeStruct((16, 128), jnp.int32),
            ),
            in_specs=[pl.BlockSpec(memory_space=pltpu.HBM)] * 5,
            out_specs=[pl.BlockSpec(memory_space=pltpu.VMEM)] * 5,
            scratch_shapes=[
                pltpu.VMEM((NY, *piece), BF16),
                pltpu.VMEM((8, TILE, V), BF16),
                pltpu.SMEM((NJ,), jnp.int32),
                pltpu.SMEM((8,), jnp.int32),
                pltpu.VMEM((1, V), jnp.int32),
                pltpu.VMEM((V, 128), jnp.int32),
                pltpu.VMEM((NY, *piece), BF16),
                pltpu.VMEM((NY, *piece), BF16),
                pltpu.VMEM((3, *piece), BF16),
                pltpu.VMEM((3, *piece), BF16),
                pltpu.VMEM((NJ, *piece), BF16),
                pltpu.VMEM((NJ, *piece), BF16),
                pltpu.VMEM((NS, *piece), BF16),
                pltpu.VMEM((NS, *piece), BF16),
                pltpu.VMEM((N_SENT, 16, V), BF16),
                pltpu.SemaphoreType.DMA((6,)),
                pltpu.SemaphoreType.DMA((1,)),
                pltpu.SemaphoreType.DMA((N_SEMS,)),
            ],
            compiler_params=pltpu.CompilerParams(
                collective_id=0, has_side_effects=True, vmem_limit_bytes=32 * 1024 * 1024
            ),
        )(*(pltpu.with_memory_space_constraint(operand, pltpu.HBM) for operand in operands))
        residual = pl.pallas_call(
            finish,
            out_shape=jax.ShapeDtypeStruct((NJ, TILE, V), F32),
            in_specs=[pl.BlockSpec(memory_space=pltpu.VMEM)] * 5,
            out_specs=pl.BlockSpec(memory_space=pltpu.HBM),
            scratch_shapes=[pltpu.VMEM((9, TILE, V), F32), pltpu.SemaphoreType.DMA((2,))],
            compiler_params=pltpu.CompilerParams(vmem_limit_bytes=16 * 1024 * 1024),
        )(*gathered)
        return residual[None]

    return jax.shard_map(
        local, mesh=mesh, in_specs=placed, out_specs=P("pair", None, "slab", None), check_vma=False
    )
```
